32 devices in a mesh: tok: 16 (over z, y, x), head: 2 (over core).
Axes of the slice: x: 2, y: 2, z: 4, core: 2. Of those that a mesh axis runs over, the one named last changes fastest.
Arguments:
- source_keys: bfloat16 [4096, 2048], P('tok', 'head'), may hold values from -6 to 6
- source_values: bfloat16 [4096, 2048], P('tok', 'head'), may hold values from -6 to 6
- queries: bfloat16 [4096, 2048], P('tok', 'head'), may hold values from -6 to 6
- fast_weights: float32 [3, 16, 128, 512], P(None, 'head'), may hold values from -0.5 to 0.5
- step_size: float32 [16], P('head'), may hold values from 0.3 to 3
- edit_mask: int32 [16], P('tok'), may hold values 0 or 1
- out_proj: bfloat16 [2048, 2048], P(None, 'head'), may hold values from -0.125 to 0.125
Outputs:
- layer_out: bfloat16 [4096, 2048], P('tok', 'head')
The draws below stay inside these ranges and needn't reach their ends.
Inputs may be any that keep to these rules, and one draw needn't show every extreme that they name: `edit_mask`: 1 marks a block of source frames whose keys and values update the fast weights, 0 a block of edited frames.
All inputs are finite; a program needn't handle non-finite values.
Results may differ from the reference program's by a relative error of at most 0.0087.
Values may be sent and summed in bfloat16 or wider, within the bound.
No kernel may reach another device: no remote copies, remote signals or barrier semaphores. Data moves between devices by JAX's collectives and lax.ppermute only.
A program may use at most 128 MiB of HBM per device.

```python
import math
import jax
import jax.numpy as jnp
from jax import lax

D = 2048
H = 16
FF = 512
DH = 128
BLOCK = 256
ITERS = 5
TOKENS = 4096
BLOCKS = 16


def touch_ends(result, key, smallest, top_value):
    longest = result.shape.index(max(result.shape))
    spots = []
    for shift in (0, 1):
        where = [jax.random.randint(jax.random.fold_in(key, axis), (), 0, length) for axis, length in enumerate(result.shape)]
        where[longest] = (where[longest] + shift) % result.shape[longest]
        spots.append(tuple(where))
    return result.at[spots[0]].set(smallest).at[spots[1]].set(top_value)


def steps_of(own_key, shape, cuts, least, largest):
    def one(position, blocks):
        heights = jax.random.uniform(jax.random.fold_in(jax.random.fold_in(own_key, 6), position), (blocks,), jnp.float32, least / len(cuts), largest / len(cuts))
        return jnp.repeat(jnp.exp(heights), shape[position] // blocks).reshape((-1,) + (1,) * (len(shape) - position - 1))

    level = one(*cuts[0])
    for cut in cuts[1:]:
        level = level * one(*cut)
    return level


def scatter_about(rng, shape, width, reach, shards=(), kind=jnp.bfloat16):
    drawn = jax.random.normal(rng, shape, jnp.float32) * width
    if len(shards) > 0:
        drawn = steps_of(rng, shape, shards, -0.22, 0.18) * drawn
    return jnp.clip(drawn, min=-reach, max=reach).astype(kind)


def setup_inputs(seed: int = 0) -> dict:
    key_list = jax.random.split(jax.random.key(seed), 8)
    source_keys = scatter_about(key_list[0], (TOKENS, D), 1.0, 6.0, ((0, 16), (1, 2)))
    source_values = scatter_about(key_list[1], (TOKENS, D), 1.0, 6.0, ((0, 16), (1, 2)))
    queries = scatter_about(key_list[2], (TOKENS, D), 1.0, 6.0, ((0, 16), (1, 2)))
    fast_weights = scatter_about(key_list[3], (3, H, DH, FF), DH ** -0.5, 0.5, ((1, 2),), jnp.float32)
    step_size = jnp.clip(jnp.exp(math.log(3.0) - 2.3025851 * jax.random.uniform(key_list[4], (H,), jnp.float32) ** steps_of(key_list[4], (H,), ((0, 2),), -0.2, 0.2)), 0.3, 3.0)
    edit_mask = touch_ends((jax.random.randint(key_list[5], (BLOCKS,), 0, 2) < 1).astype(jnp.int32), jax.random.fold_in(key_list[5], 1), 0, 1)
    out_proj = scatter_about(key_list[6], (D, D), D ** -0.5, 0.125, ((1, 2),))
    return {"source_keys": source_keys, "source_values": source_values, "queries": queries, "fast_weights": fast_weights, "step_size": step_size, "edit_mask": edit_mask, "out_proj": out_proj}


coef_a = 3.4445
coef_b = -4.775
coef_c = 2.0315
highest = lax.Precision.HIGHEST

def silu_grad(preact):
    sigmoid_value = jax.nn.sigmoid(preact)
    return sigmoid_value * (1.0 + preact * (1.0 - sigmoid_value))

def orthogonalize(gradients):
    scaling = lax.rsqrt(lax.optimization_barrier(jnp.sum(gradients * gradients, axis=(-2, -1), keepdims=True)) + 1e-06)
    iterate = gradients * scaling
    for sweeps in range(ITERS):
        gram_matrix = jnp.einsum('...if,...jf->...ij', iterate, iterate, precision=highest)
        polynomial = coef_b * gram_matrix + coef_c * jnp.einsum('...ij,...jk->...ik', gram_matrix, gram_matrix, precision=highest)
        iterate = coef_a * iterate + jnp.einsum('...ij,...jf->...if', polynomial, iterate, precision=highest)
    return iterate

def renormalize(previous, proposed):
    old_norm = jnp.sqrt(lax.optimization_barrier(jnp.sum(previous * previous, axis=-2, keepdims=True)) + 1e-06)
    new_norm = jnp.sqrt(lax.optimization_barrier(jnp.sum(proposed * proposed, axis=-2, keepdims=True)) + 1e-06)
    return proposed * (old_norm / new_norm)

def head_step(operands):
    keys_head, values_head, query_head, weights, rate_head = operands
    weights_low = weights.astype(jnp.bfloat16)
    gate_pre = jnp.dot(keys_head, weights_low[0], preferred_element_type=jnp.float32)
    up_pre = jnp.dot(keys_head, weights_low[2], preferred_element_type=jnp.float32)
    hidden = (jax.nn.silu(gate_pre) * up_pre).astype(jnp.bfloat16)
    back_grad = jnp.dot(values_head, weights_low[1], preferred_element_type=jnp.float32)
    gate_grad = (back_grad * up_pre * silu_grad(gate_pre)).astype(jnp.bfloat16)
    up_grad = (back_grad * jax.nn.silu(gate_pre)).astype(jnp.bfloat16)
    grad_gate = jnp.dot(keys_head.T, gate_grad, preferred_element_type=jnp.float32)
    grad_down = jnp.dot(values_head.T, hidden, preferred_element_type=jnp.float32)
    grad_up = jnp.dot(keys_head.T, up_grad, preferred_element_type=jnp.float32)
    gradients = jnp.stack([grad_gate, grad_down, grad_up])
    directions = orthogonalize(gradients)
    updated = renormalize(weights, weights + rate_head * directions).astype(jnp.bfloat16)
    read_gate = jnp.dot(query_head, updated[0], preferred_element_type=jnp.float32)
    read_up = jnp.dot(query_head, updated[2], preferred_element_type=jnp.float32)
    read_hidden = (jax.nn.silu(read_gate) * read_up).astype(jnp.bfloat16)
    return jnp.dot(read_hidden, updated[1].T, preferred_element_type=jnp.float32).astype(jnp.bfloat16)

def reference(source_keys, source_values, queries, fast_weights, step_size, edit_mask, out_proj):
    token_mask = jnp.repeat(edit_mask, BLOCK).astype(jnp.bfloat16)
    keys_heads = jnp.moveaxis(source_keys.reshape(TOKENS, H, DH), 1, 0)
    masked_values = source_values.reshape(TOKENS, H, DH) * token_mask[:, None, None]
    values_heads = jnp.moveaxis(masked_values, 1, 0)
    query_heads = jnp.moveaxis(queries.reshape(TOKENS, H, DH), 1, 0)
    weight_heads = jnp.moveaxis(fast_weights, 1, 0)
    reads = lax.map(head_step, (keys_heads, values_heads, query_heads, weight_heads, step_size))
    read_all = jnp.moveaxis(reads, 0, 1).reshape(TOKENS, D)
    projected = jnp.dot(read_all, out_proj, preferred_element_type=jnp.float32)
    return jax.nn.silu(projected).astype(jnp.bfloat16)
```

```python
import functools

import jax
import jax.numpy as jnp
from jax import lax
from jax.experimental import pallas as pl
from jax.experimental.pallas import tpu as pltpu
from jax.sharding import PartitionSpec as P

ITERS = 5
COEF_A = 3.4445
COEF_B = -4.775
COEF_C = 2.0315
BF16 = jnp.bfloat16
F32 = jnp.float32
NN = (((1,), (0,)), ((), ()))
NT = (((1,), (1,)), ((), ()))
TN = (((0,), (0,)), ((), ()))


def dot(a, b, dims=NN):
    return lax.dot_general(a, b, dims, preferred_element_type=F32)


def halves(x):
    high = x.astype(BF16)
    return high, (x - high.astype(F32)).astype(BF16)


def dot3(a, b, dims=NN):
    (ah, al), (bh, bl) = a, b
    return dot(ah, bh, dims) + (dot(ah, bl, dims) + dot(al, bh, dims))


def sigmoid(x):
    return 0.5 + 0.5 * jnp.tanh(0.5 * x)


def gradient_kernel(chunk, recv_ref, weights_ref, grads_ref):
    sources, _, sub, dh = recv_ref.shape
    ff = weights_ref.shape[-1]
    gate_up = jnp.concatenate([weights_ref[0], weights_ref[2]], axis=1).astype(BF16)
    down = weights_ref[1].astype(BF16)
    grads_ref[...] = jnp.zeros_like(grads_ref)

    def step(i, _):
        rows = pl.ds(i * chunk, chunk)
        keys = recv_ref[rows, 0].reshape(chunk * sub, dh)
        values = recv_ref[rows, 1].reshape(chunk * sub, dh)
        pre = dot(keys, gate_up)
        gate, up = pre[:, :ff], pre[:, ff:]
        back = dot(values, down)
        sig = sigmoid(gate)
        act = gate * sig
        hidden = (act * up).astype(BF16)
        gate_grad = (back * up * (sig + act * (1.0 - sig))).astype(BF16)
        up_grad = (back * act).astype(BF16)
        grads_ref[0] += dot(keys, gate_grad, TN)
        grads_ref[1] += dot(values, hidden, TN)
        grads_ref[2] += dot(keys, up_grad, TN)
        return 0

    lax.fori_loop(0, sources // chunk, step, 0)


def update_kernel(chunk, iters, *refs):
    parts, (weights_ref, rate_ref, query_ref, read_ref, new_ref) = refs[:-5], refs[-5:]
    sources, sub, dh = query_ref.shape
    kinds, _, ff = weights_ref.shape
    rate = rate_ref[0:1, :]
    iterates = []
    for m in range(kinds):
        grad = parts[0][m]
        for part in parts[1:]:
            grad = grad + part[m]
        iterates.append(grad * lax.rsqrt(jnp.sum(grad * grad) + 1e-06))
    for _ in range(iters):
        split = [halves(x) for x in iterates]
        gram = [dot3(s, s, NT) for s in split]
        gram_split = [halves(a) for a in gram]
        square = [dot3(s, s) for s in gram_split]
        poly = [halves(COEF_B * a + COEF_C * b) for a, b in zip(gram, square)]
        iterates = [COEF_A * x + dot3(p, s) for x, p, s in zip(iterates, poly, split)]
    for m in range(kinds):
        old = weights_ref[m]
        new = old + rate * iterates[m]
        old_norm = jnp.sqrt(jnp.sum(old * old, axis=0, keepdims=True) + 1e-06)
        new_norm = jnp.sqrt(jnp.sum(new * new, axis=0, keepdims=True) + 1e-06)
        new_ref[m] = (new * (old_norm / new_norm)).astype(BF16)
    gate_up = jnp.concatenate([new_ref[0], new_ref[2]], axis=1)
    down = new_ref[1]

    def step(i, _):
        rows = pl.ds(i * chunk, chunk)
        pre = dot(query_ref[rows].reshape(chunk * sub, dh), gate_up)
        gate, up = pre[:, :ff], pre[:, ff:]
        hidden = (gate * sigmoid(gate) * up).astype(BF16)
        read = dot(hidden, down, NT).astype(BF16)
        read_ref[rows] = read.reshape(chunk, sub, dh)
        return 0

    lax.fori_loop(0, sources // chunk, step, 0)


def project_kernel(place_ref, *refs):
    reads, (weight_ref, out_ref) = refs[:-2], refs[-2:]
    heads, sub, _ = reads[0].shape
    for s, read in enumerate(reads):
        flat = jnp.concatenate([read[i] for i in range(heads)], axis=1)
        value = dot(flat, weight_ref[...])
        out_ref[pl.ds(pl.multiple_of(place_ref[s] * sub, sub), sub), :] = (
            value * sigmoid(value)
        ).astype(BF16)


def call(kernel, out_shape, args, scalars=0, scratch=(), limit=32):
    specs = [pl.BlockSpec(memory_space=pltpu.SMEM)] * scalars
    specs += [pl.BlockSpec(memory_space=pltpu.VMEM)] * (len(args) - scalars)
    return pl.pallas_call(
        kernel,
        out_shape=out_shape,
        in_specs=specs,
        out_specs=pl.BlockSpec(memory_space=pltpu.VMEM),
        scratch_shapes=list(scratch),
        compiler_params=pltpu.CompilerParams(vmem_limit_bytes=limit * 2**20),
    )(*args)


def on_device(tok_size, head_size, keys, values, queries, fast_weights, step_size, edit_mask, out_proj):
    tokens = keys.shape[0]
    kinds, local_heads, dh, ff = fast_weights.shape
    heads = local_heads * head_size
    sub = tokens // head_size
    column = lax.axis_index("head")
    my_head = lax.axis_index("tok") % heads
    groups = [[g * heads + i for i in range(heads)] for g in range(tok_size // heads)]
    whole = len(groups) == 1

    def send(x, shift):
        return lax.ppermute(x, "head", [(i, (i + shift) % head_size) for i in range(head_size)])

    def shuffle(x):
        if whole:
            return lax.all_to_all(x, "tok", 0, 0, tiled=True)
        return lax.all_to_all(x, "tok", 0, 0, tiled=True, axis_index_groups=groups)

    def by_owner(pieces):
        ordered = []
        for owner in range(head_size):
            value = pieces[0]
            for s in range(1, head_size):
                value = jnp.where((column - owner) % head_size == s, pieces[s], value)
            ordered.append(value)
        return jnp.concatenate(ordered, axis=0)

    def swap(x):
        pieces = []
        for s in range(head_size):
            piece = lax.dynamic_index_in_dim(x, (column + s) % head_size, 0, keepdims=False)
            pieces.append(send(piece, s) if s else piece)
        return by_owner(pieces)

    def by_part(x):
        return x.reshape(head_size, sub, local_heads, dh).transpose(0, 2, 1, 3)

    mask = jnp.repeat(edit_mask, tokens // edit_mask.shape[0]).astype(BF16)
    pairs = jnp.stack([by_part(keys), by_part(values * mask[:, None])], axis=2)
    received = shuffle(swap(pairs))
    asked = shuffle(swap(by_part(queries)))

    slot = my_head % local_heads
    own = lax.dynamic_index_in_dim(fast_weights, slot, 1, keepdims=False).reshape(kinds * dh, ff)
    rate = jnp.broadcast_to(lax.dynamic_index_in_dim(step_size, slot, 0, keepdims=False), (8, ff))
    own = jnp.concatenate([own, rate], axis=0)
    mine = own
    for s in range(1, head_size):
        mine = jnp.where((column - my_head // local_heads) % head_size == s, send(own, s), mine)
    weights = mine[: kinds * dh].reshape(kinds, dh, ff)
    rate = mine[kinds * dh :]

    chunk = 4 if heads % 4 == 0 else 1
    partial = call(
        functools.partial(gradient_kernel, chunk),
        jax.ShapeDtypeStruct((kinds, dh, ff), F32),
        (received, weights),
    )
    if not whole:
        others = [[g * heads + i for g in range(tok_size // heads)] for i in range(heads)]
        partial = lax.psum(partial, "tok", axis_index_groups=others)
    if head_size == 2:
        partials = [partial, send(partial, 1)]
    else:
        partials = [lax.psum(partial, "head")]
    read = call(
        functools.partial(update_kernel, chunk, ITERS),
        jax.ShapeDtypeStruct((heads, sub, dh), BF16),
        (*partials, weights, rate, asked),
        scratch=[pltpu.VMEM((kinds, dh, ff), BF16)],
    )
    reads = shuffle(read)
    pieces = [send(reads, s) if s else reads for s in range(head_size)]
    places = (column - jnp.arange(head_size, dtype=jnp.int32)) % head_size
    return call(
        project_kernel,
        jax.ShapeDtypeStruct((tokens, out_proj.shape[1]), BF16),
        (places, *pieces, out_proj),
        scalars=1,
    )


def solution(mesh):
    sizes = dict(mesh.shape)
    in_specs = (
        P("tok", "head"),
        P("tok", "head"),
        P("tok", "head"),
        P(None, "head", None, None),
        P("head"),
        P("tok"),
        P(None, "head"),
    )
    return jax.shard_map(
        functools.partial(on_device, sizes["tok"], sizes["head"]),
        mesh=mesh,
        in_specs=in_specs,
        out_specs=P("tok", "head"),
        check_vma=False,
    )
```

```python
import functools

import jax
import jax.numpy as jnp
from jax import lax
from jax.experimental import pallas as pl
from jax.experimental.pallas import tpu as pltpu
from jax.sharding import PartitionSpec as P

ITERS = 5
COEF_A = 3.4445
COEF_B = -4.775
COEF_C = 2.0315
BF16 = jnp.bfloat16
F32 = jnp.float32
NN = (((1,), (0,)), ((), ()))
NT = (((1,), (1,)), ((), ()))
TN = (((0,), (0,)), ((), ()))


def dot(a, b, dims=NN):
    return lax.dot_general(a, b, dims, preferred_element_type=F32)


def halves(x):
    high = x.astype(BF16)
    return high, (x - high.astype(F32)).astype(BF16)


def dot3(a, b, dims=NN):
    (ah, al), (bh, bl) = a, b
    return dot(ah, bh, dims) + (dot(ah, bl, dims) + dot(al, bh, dims))


def sigmoid(x):
    return 0.5 + 0.5 * jnp.tanh(0.5 * x)


def gradient_kernel(chunk, recv_ref, weights_ref, grads_ref, low_ref):
    sources, _, sub, dh = recv_ref.shape
    ff = weights_ref.shape[-1]
    gate_up = jnp.concatenate([weights_ref[0], weights_ref[2]], axis=1).astype(BF16)
    down = weights_ref[1].astype(BF16)
    grads_ref[...] = jnp.zeros_like(grads_ref)

    def step(i, _):
        rows = pl.ds(i * chunk, chunk)
        keys = recv_ref[rows, 0].reshape(chunk * sub, dh)
        values = recv_ref[rows, 1].reshape(chunk * sub, dh)
        pre = dot(keys, gate_up)
        gate, up = pre[:, :ff], pre[:, ff:]
        back = dot(values, down)
        sig = sigmoid(gate)
        act = gate * sig
        hidden = (act * up).astype(BF16)
        gate_grad = (back * up * (sig + act * (1.0 - sig))).astype(BF16)
        up_grad = (back * act).astype(BF16)
        grads_ref[0] += dot(keys, gate_grad, TN)
        grads_ref[1] += dot(values, hidden, TN)
        grads_ref[2] += dot(keys, up_grad, TN)
        return 0

    lax.fori_loop(0, sources // chunk, step, 0)
    low_ref[...] = grads_ref[...].astype(BF16)


def update_kernel(chunk, iters, rate_ref, *refs):
    parts, (weights_ref, query_ref, read_ref, new_ref) = refs[:-4], refs[-4:]
    sources, sub, dh = query_ref.shape
    kinds, _, ff = weights_ref.shape
    rate = rate_ref[0]
    iterates = []
    for m in range(kinds):
        grad = parts[0][m]
        for part in parts[1:]:
            grad = grad + part[m].astype(F32)
        iterates.append(grad * lax.rsqrt(jnp.sum(grad * grad) + 1e-06))
    for _ in range(iters):
        split = [halves(x) for x in iterates]
        gram = [dot3(s, s, NT) for s in split]
        gram_split = [halves(a) for a in gram]
        square = [dot3(s, s) for s in gram_split]
        poly = [halves(COEF_B * a + COEF_C * b) for a, b in zip(gram, square)]
        iterates = [COEF_A * x + dot3(p, s) for x, p, s in zip(iterates, poly, split)]
    for m in range(kinds):
        old = weights_ref[m]
        new = old + rate * iterates[m]
        old_norm = jnp.sqrt(jnp.sum(old * old, axis=0, keepdims=True) + 1e-06)
        new_norm = jnp.sqrt(jnp.sum(new * new, axis=0, keepdims=True) + 1e-06)
        new_ref[m] = (new * (old_norm / new_norm)).astype(BF16)
    gate_up = jnp.concatenate([new_ref[0], new_ref[2]], axis=1)
    down = new_ref[1]

    def step(i, _):
        rows = pl.ds(i * chunk, chunk)
        pre = dot(query_ref[rows].reshape(chunk * sub, dh), gate_up)
        gate, up = pre[:, :ff], pre[:, ff:]
        hidden = (gate * sigmoid(gate) * up).astype(BF16)
        read = dot(hidden, down, NT).astype(BF16)
        read_ref[rows] = read.reshape(chunk, sub, dh)
        return 0

    lax.fori_loop(0, sources // chunk, step, 0)


def project_own_kernel(place_ref, read_ref, weight_ref, sum_ref):
    heads = read_ref.shape[0]
    flat = jnp.concatenate([read_ref[i] for i in range(heads)], axis=1)
    depth = flat.shape[1]
    rows = pl.ds(pl.multiple_of(place_ref[0] * depth, depth), depth)
    sum_ref[...] = dot(flat, weight_ref[rows, :])


def project_rest_kernel(place_ref, sum_ref, *refs):
    reads, (weight_ref, out_ref) = refs[:-2], refs[-2:]
    heads = reads[0].shape[0]
    value = sum_ref[...]
    for s, read in enumerate(reads):
        flat = jnp.concatenate([read[i] for i in range(heads)], axis=1)
        depth = flat.shape[1]
        rows = pl.ds(pl.multiple_of(place_ref[s + 1] * depth, depth), depth)
        value = value + dot(flat, weight_ref[rows, :])
    out_ref[...] = (value * sigmoid(value)).astype(BF16)


def call(kernel, out_shape, args, scalars=0, scratch=(), limit=32):
    specs = [pl.BlockSpec(memory_space=pltpu.SMEM)] * scalars
    specs += [pl.BlockSpec(memory_space=pltpu.VMEM)] * (len(args) - scalars)
    return pl.pallas_call(
        kernel,
        out_shape=out_shape,
        in_specs=specs,
        out_specs=jax.tree.map(lambda _: pl.BlockSpec(memory_space=pltpu.VMEM), out_shape),
        scratch_shapes=list(scratch),
        compiler_params=pltpu.CompilerParams(vmem_limit_bytes=limit * 2**20),
    )(*args)


def on_device(tok_size, head_size, keys, values, queries, fast_weights, step_size, edit_mask, out_proj):
    tokens = keys.shape[0]
    kinds, heads, dh, ff = fast_weights.shape
    column = lax.axis_index("head")
    slot = lax.axis_index("tok") % heads
    count = tok_size // heads
    groups = [[g * heads + i for i in range(heads)] for g in range(count)]

    def shuffle(x):
        return lax.all_to_all(x, "tok", 0, 0, tiled=True, axis_index_groups=groups)

    def by_head(x):
        return x.reshape(tokens, heads, dh).transpose(1, 0, 2)

    mask = jnp.repeat(edit_mask, tokens // edit_mask.shape[0]).astype(BF16)
    received = shuffle(jnp.stack([by_head(keys), by_head(values * mask[:, None])], axis=1))
    weights = lax.dynamic_index_in_dim(fast_weights, slot, 1, keepdims=False)
    rate = lax.dynamic_slice_in_dim(step_size, slot, 1)

    chunk = 2 if heads % 2 == 0 else 1
    partial, low = call(
        functools.partial(gradient_kernel, chunk),
        (jax.ShapeDtypeStruct((kinds, dh, ff), F32), jax.ShapeDtypeStruct((kinds, dh, ff), BF16)),
        (received, weights),
    )
    low, packed = lax.optimization_barrier((low, by_head(queries)))
    if count == 1:
        partials = [partial]
    elif count == 2:
        partials = [partial, lax.ppermute(low, "tok", [(i, (i + heads) % tok_size) for i in range(tok_size)])]
    else:
        others = [[g * heads + i for g in range(count)] for i in range(heads)]
        partials = [lax.psum(partial, "tok", axis_index_groups=others)]
    asked = shuffle(packed)
    read = call(
        functools.partial(update_kernel, chunk, ITERS),
        jax.ShapeDtypeStruct((heads, tokens, dh), BF16),
        (rate, *partials, weights, asked),
        scalars=1,
        scratch=[pltpu.VMEM((kinds, dh, ff), BF16)],
    )
    reads = shuffle(read)
    pieces = [
        lax.ppermute(reads, "head", [(i, (i + s) % head_size) for i in range(head_size)])
        for s in range(1, head_size)
    ]
    places = (column - jnp.arange(head_size, dtype=jnp.int32)) % head_size
    columns = out_proj.shape[1]
    own = call(
        project_own_kernel,
        jax.ShapeDtypeStruct((tokens, columns), F32),
        (places, reads, out_proj),
        scalars=1,
    )
    return call(
        project_rest_kernel,
        jax.ShapeDtypeStruct((tokens, columns), BF16),
        (places, own, *pieces, out_proj),
        scalars=1,
    )


def solution(mesh):
    sizes = dict(mesh.shape)
    in_specs = (
        P("tok", "head"),
        P("tok", "head"),
        P("tok", "head"),
        P(None, "head", None, None),
        P("head"),
        P("tok"),
        P(None, "head"),
    )
    return jax.shard_map(
        functools.partial(on_device, sizes["tok"], sizes["head"]),
        mesh=mesh,
        in_specs=in_specs,
        out_specs=P("tok", "head"),
        check_vma=False,
    )
```

```python
import functools

import jax
import jax.numpy as jnp
from jax import lax
from jax.experimental import pallas as pl
from jax.experimental.pallas import tpu as pltpu
from jax.sharding import PartitionSpec as P

ITERS = 5
COEF_A = 3.4445
COEF_B = -4.775
COEF_C = 2.0315
BF16 = jnp.bfloat16
F32 = jnp.float32
LANES = 128
KINDS = 3
NN = (((1,), (0,)), ((), ()))
NT = (((1,), (1,)), ((), ()))
TN = (((0,), (0,)), ((), ()))


def dot(a, b, dims=NN):
    return lax.dot_general(a, b, dims, preferred_element_type=F32)


def halves(x):
    high = x.astype(BF16)
    return high, (x - high.astype(F32)).astype(BF16)


def sigmoid(x):
    return 0.5 + 0.5 * jnp.tanh(0.5 * x)


def pack_kernel(mask_ref, keys_ref, values_ref, pairs_ref, kept_ref, mask_kept, in_sem, out_sem, mask_sem):
    heads, _, tokens, dh = pairs_ref.shape
    blocks = mask_ref.shape[1]
    length = tokens // blocks
    sources = (keys_ref, values_ref)
    mask_copy = pltpu.make_async_copy(mask_ref, mask_kept, mask_sem)
    mask_copy.start()
    loads, stores = [], []
    for i in range(heads):
        for p in range(2):
            loads.append(
                pltpu.make_async_copy(
                    sources[p].at[:, pl.ds(i * dh, dh)], kept_ref.at[i, p], in_sem.at[i, p]
                )
            )
            stores.append(
                pltpu.make_async_copy(kept_ref.at[i, p], pairs_ref.at[i, p], out_sem.at[i, p])
            )
    for load in loads:
        load.start()
    mask_copy.wait()
    for i in range(heads):
        for p in range(2):
            loads[2 * i + p].wait()
            if p == 1:
                for b in range(blocks):
                    rows = pl.ds(b * length, length)
                    kept = kept_ref[i, 1, rows].astype(F32) * mask_kept[:, b : b + 1].astype(F32)
                    kept_ref[i, 1, rows] = kept.astype(BF16)
            stores[2 * i + p].start()
    for store in stores:
        store.wait()


def gradient_kernel(chunk, start, recv_ref, weights_ref, grads_ref, coded_ref):
    sources, _, sub, dh = recv_ref.shape
    ff = grads_ref.shape[-1]
    units = pl.ds(start, ff)
    gate_up = jnp.concatenate([weights_ref[0, :, units], weights_ref[2, :, units]], axis=1).astype(BF16)
    down = weights_ref[1, :, units].astype(BF16)
    for i in range(0, sources, chunk):
        rows = pl.ds(i, chunk)
        keys = recv_ref[rows, 0].reshape(chunk * sub, dh)
        values = recv_ref[rows, 1].reshape(chunk * sub, dh)
        pre = dot(keys, gate_up)
        gate, up = pre[:, :ff], pre[:, ff:]
        back = dot(values, down)
        sig = sigmoid(gate)
        act = gate * sig
        hidden = (act * up).astype(BF16)
        gate_grad = (back * up * (sig + act * (1.0 - sig))).astype(BF16)
        up_grad = (back * act).astype(BF16)
        sums = dot(keys.T, jnp.concatenate([gate_grad, up_grad], axis=1))
        sums = (sums[:, :ff], dot(values.T, hidden), sums[:, ff:])
        for m, value in enumerate(sums):
            grads_ref[m] = value if i == 0 else grads_ref[m] + value
    encode(grads_ref, coded_ref)


def encode(grads_ref, coded_ref):
    kinds, dh, ff = grads_ref.shape
    powers = []
    for m in range(kinds):
        for c in range(ff // LANES):
            block = grads_ref[m, :, c * LANES : (c + 1) * LANES]
            top = jnp.max(jnp.abs(block), axis=0, keepdims=True)
            power = jnp.floor(jnp.log2(jnp.maximum(top, 1e-30))) - 14.0
            code = jnp.clip(jnp.round(block * jnp.exp2(-power)), -32767.0, 32767.0)
            coded_ref[pl.ds(len(powers) * dh, dh)] = code.astype(jnp.int32).astype(jnp.int16)
            powers.append(power)
    rest = coded_ref.shape[0] - len(powers) * dh
    powers += [jnp.zeros_like(powers[0])] * (rest - len(powers))
    power = jnp.concatenate(powers, axis=0)
    coded_ref[pl.ds(coded_ref.shape[0] - rest, rest)] = power.astype(jnp.int32).astype(jnp.int16)


def decode(coded_ref, m, dh, ff):
    width = ff // LANES
    rest = code_rows(KINDS * width)
    power = coded_ref[pl.ds(coded_ref.shape[0] - rest, rest)].astype(jnp.int32).astype(F32)
    blocks = []
    for c in range(width):
        i = m * width + c
        code = coded_ref[pl.ds(i * dh, dh)].astype(jnp.int32).astype(F32)
        blocks.append(code * jnp.exp2(power[i : i + 1]))
    return jnp.concatenate(blocks, axis=1)


def code_rows(columns):
    return -(-columns // 16) * 16


def product(a, b):
    (ah, al), (bh, bl) = a, b
    return dot(jnp.concatenate([ah, al], axis=1), jnp.concatenate([bh, bh], axis=0)) + dot(ah, bl)


def newton_schulz(iterates, iters):
    for _ in range(iters):
        split = [halves(x) for x in iterates]
        gram = []
        for high, low in split:
            both = dot(high, jnp.concatenate([high, low], axis=0), NT)
            size = high.shape[0]
            cross = both[:, size:]
            gram.append(both[:, :size] + (cross + cross.T))
        gram_split = [halves(a) for a in gram]
        square = []
        for high, low in gram_split:
            wide = jnp.concatenate([high, low], axis=1)
            under = jnp.concatenate([high, jnp.zeros_like(high)], axis=1)
            both = dot(wide, jnp.concatenate([wide, under], axis=0))
            size = high.shape[0]
            square.append(both[:, :size] + both[:, size:])
        poly = [halves(COEF_B * a + COEF_C * b) for a, b in zip(gram, square)]
        iterates = [COEF_A * x + product(p, s) for x, p, s in zip(iterates, poly, split)]
    return iterates


def update_kernel(iters, coded, slot_ref, rate_ref, *refs):
    weights_ref, new_ref = refs[-2:]
    kinds, dh, ff = weights_ref.shape
    rate = rate_ref[slot_ref[0]]
    partials, others = refs[:-2], ()
    if coded:
        partials, others = refs[: len(refs) // 2 - 1], refs[len(refs) // 2 - 1 : -2]
    iterates = []
    for m in range(kinds):
        blocks = [partial[m] for partial in partials]
        if coded:
            blocks = [
                block + decode(other, m, dh, block.shape[-1])
                for block, other in zip(blocks, others)
            ]
        grad = jnp.concatenate(blocks, axis=1)
        iterates.append(grad * lax.rsqrt(jnp.sum(grad * grad) + 1e-06))
    iterates = newton_schulz(iterates, iters)
    for m in range(kinds):
        old = weights_ref[m]
        new = old + rate * iterates[m]
        old_norm = jnp.sqrt(jnp.sum(old * old, axis=0, keepdims=True) + 1e-06)
        new_norm = jnp.sqrt(jnp.sum(new * new, axis=0, keepdims=True) + 1e-06)
        new_ref[m] = (new * (old_norm / new_norm)).astype(BF16)


def read_kernel(chunk, new_ref, query_ref, read_ref):
    sources, sub, dh = query_ref.shape
    ff = new_ref.shape[-1]
    gate_up = jnp.concatenate([new_ref[0], new_ref[2]], axis=1)
    down = new_ref[1]

    def step(i, _):
        rows = pl.ds(i * chunk, chunk)
        pre = dot(query_ref[rows].reshape(chunk * sub, dh), gate_up)
        gate, up = pre[:, :ff], pre[:, ff:]
        hidden = (gate * sigmoid(gate) * up).astype(BF16)
        read = dot(hidden, down, NT).astype(BF16)
        read_ref[rows] = read.reshape(chunk, sub, dh)
        return 0

    lax.fori_loop(0, sources // chunk, step, 0)


def flat_heads(read_ref):
    return jnp.concatenate([read_ref[i] for i in range(read_ref.shape[0])], axis=1)


def project_own_kernel(column_ref, read_ref, weight_ref, sum_ref, *refs):
    rest_refs, (own_ref, sems) = refs[:-2], refs[-2:]
    depth, columns = own_ref.shape
    size = weight_ref.shape[0] // depth
    copies = []
    for s, target in enumerate((own_ref, *rest_refs)):
        rows = pl.ds(pl.multiple_of(lax.rem(column_ref[0] + size - s, size) * depth, depth), depth)
        copies.append(pltpu.make_async_copy(weight_ref.at[rows], target, sems.at[s]))
        copies[-1].start()
    copies[0].wait()
    sum_ref[...] = dot(flat_heads(read_ref), own_ref[...])
    for copy in copies[1:]:
        copy.wait()


def project_rest_kernel(sum_ref, *refs):
    reads, weights, out_ref = refs[: len(refs) // 2], refs[len(refs) // 2 : -1], refs[-1]
    value = sum_ref[...]
    for read, weight in zip(reads, weights):
        value = value + dot(flat_heads(read), weight[...])
    out_ref[...] = (value * sigmoid(value)).astype(BF16)


def call(kernel, out_shape, args, scalars=0, flops=None, limit=12, hbm=(), scratch=()):
    specs = [pl.BlockSpec(memory_space=pltpu.SMEM)] * scalars
    specs += [
        pl.BlockSpec(memory_space=pl.ANY if i in hbm else pltpu.VMEM)
        for i in range(scalars, len(args))
    ]
    cost = None
    if flops is not None:
        cost = pl.CostEstimate(flops=flops, bytes_accessed=2**20, transcendentals=0)
    return pl.pallas_call(
        kernel,
        out_shape=out_shape,
        in_specs=specs,
        out_specs=jax.tree.map(
            lambda _: pl.BlockSpec(memory_space=pl.ANY if -1 in hbm else pltpu.VMEM), out_shape
        ),
        scratch_shapes=list(scratch),
        compiler_params=pltpu.CompilerParams(vmem_limit_bytes=limit * 2**20),
        cost_estimate=cost,
    )(*args)


def on_device(tok_size, head_size, keys, values, queries, fast_weights, step_size, edit_mask, out_proj):
    tokens = keys.shape[0]
    kinds, heads, dh, ff = fast_weights.shape
    column = lax.axis_index("head")
    slot = lax.axis_index("tok") % heads
    count = tok_size // heads
    groups = [[g * heads + i for i in range(heads)] for g in range(count)]
    struct = jax.ShapeDtypeStruct

    def shuffle(x):
        return lax.all_to_all(x, "tok", 0, 0, tiled=True, axis_index_groups=groups)

    pairs = call(
        pack_kernel,
        struct((heads, 2, tokens, dh), BF16),
        (edit_mask[None], keys, values),
        hbm=(-1, 0, 1, 2),
        limit=60,
        scratch=[
            pltpu.VMEM((heads, 2, tokens, dh), BF16),
            pltpu.VMEM((1, *edit_mask.shape), edit_mask.dtype),
            pltpu.SemaphoreType.DMA((heads, 2)),
            pltpu.SemaphoreType.DMA((heads, 2)),
            pltpu.SemaphoreType.DMA,
        ],
    )
    received = shuffle(pairs)
    weights = lax.dynamic_index_in_dim(fast_weights, slot, 1, keepdims=False)
    chunk = max(c for c in (1, 2, 4) if heads % c == 0)
    split = 2 if ff % (2 * LANES) == 0 else 1
    width = ff // split
    partials, coded = [], []
    for start in range(0, ff, width):
        rows = kinds * dh * width // LANES + code_rows(kinds * width // LANES)
        partial, code = call(
            functools.partial(gradient_kernel, max(1, chunk // 2), start),
            (struct((kinds, dh, width), F32), struct((rows, LANES), jnp.int16)),
            (received, weights),
            flops=2**32,
            limit=16,
        )
        partials.append(partial)
        code, received = lax.optimization_barrier((code, received))
        coded.append(code)

    packed = queries.reshape(tokens, heads, dh).transpose(1, 0, 2)
    coded[-1], packed = lax.optimization_barrier((coded[-1], packed))
    if count == 2:
        turn = [(i, (i + heads) % tok_size) for i in range(tok_size)]
        parts = (*partials, *[lax.ppermute(code, "tok", turn) for code in coded])
    else:
        others = [[g * heads + i for g in range(count)] for i in range(heads)]
        parts = lax.psum(tuple(partials), "tok", axis_index_groups=others)
    asked = shuffle(packed)
    new = call(
        functools.partial(update_kernel, ITERS, count == 2),
        struct((kinds, dh, ff), BF16),
        (slot.reshape(1), step_size, *parts, weights),
        scalars=2,
        flops=2**33,
    )
    read = call(
        functools.partial(read_kernel, chunk), struct((heads, tokens, dh), BF16), (new, asked), limit=16
    )

    reads = shuffle(read)
    pieces = [
        lax.ppermute(reads, "head", [(i, (i + s) % head_size) for i in range(head_size)])
        for s in range(1, head_size)
    ]
    columns = out_proj.shape[1]
    depth = heads * dh
    own, *rest = call(
        project_own_kernel,
        (
            struct((tokens, columns), F32),
            *[struct((depth, columns), BF16) for _ in range(1, head_size)],
        ),
        (column.reshape(1), reads, out_proj),
        scalars=1,
        hbm=(2,),
        limit=49,
        scratch=[pltpu.VMEM((depth, columns), BF16), pltpu.SemaphoreType.DMA((head_size,))],
    )
    return call(
        project_rest_kernel, struct((tokens, columns), BF16), (own, *pieces, *rest)
    )


def solution(mesh):
    sizes = dict(mesh.shape)
    in_specs = (
        P("tok", "head"),
        P("tok", "head"),
        P("tok", "head"),
        P(None, "head", None, None),
        P("head"),
        P("tok"),
        P(None, "head"),
    )
    return jax.shard_map(
        functools.partial(on_device, sizes["tok"], sizes["head"]),
        mesh=mesh,
        in_specs=in_specs,
        out_specs=P("tok", "head"),
        check_vma=False,
    )
```

```python
import functools

import jax
import jax.numpy as jnp
from jax import lax
from jax.experimental import pallas as pl
from jax.experimental.pallas import tpu as pltpu
from jax.sharding import PartitionSpec as P

ITERS = 5
COEF_A = 3.4445
COEF_B = -4.775
COEF_C = 2.0315
BF16 = jnp.bfloat16
F32 = jnp.float32
LANES = 128
KINDS = 3
NN = (((1,), (0,)), ((), ()))
NT = (((1,), (1,)), ((), ()))
TN = (((0,), (0,)), ((), ()))


def dot(a, b, dims=NN):
    return lax.dot_general(a, b, dims, preferred_element_type=F32)


def halves(x):
    high = x.astype(BF16)
    return high, (x - high.astype(F32)).astype(BF16)


def sigmoid(x):
    return 0.5 + 0.5 * jnp.tanh(0.5 * x)


def pack_kernel(mask_ref, keys_ref, values_ref, pairs_ref, kept_ref, mask_kept, in_sem, out_sem, mask_sem):
    heads, _, tokens, dh = pairs_ref.shape
    blocks = mask_ref.shape[1]
    length = tokens // blocks
    sources = (keys_ref, values_ref)
    mask_copy = pltpu.make_async_copy(mask_ref, mask_kept, mask_sem)
    mask_copy.start()
    loads, stores = [], []
    for i in range(heads):
        for p in range(2):
            loads.append(
                pltpu.make_async_copy(
                    sources[p].at[:, pl.ds(i * dh, dh)], kept_ref.at[i, p], in_sem.at[i, p]
                )
            )
            stores.append(
                pltpu.make_async_copy(kept_ref.at[i, p], pairs_ref.at[i, p], out_sem.at[i, p])
            )
    for load in loads:
        load.start()
    mask_copy.wait()
    for i in range(heads):
        for p in range(2):
            loads[2 * i + p].wait()
            if p == 1:
                for b in range(blocks):
                    rows = pl.ds(b * length, length)
                    kept = kept_ref[i, 1, rows].astype(F32) * mask_kept[:, b : b + 1].astype(F32)
                    kept_ref[i, 1, rows] = kept.astype(BF16)
            stores[2 * i + p].start()
    for store in stores:
        store.wait()


def gradient_kernel(chunk, start, recv_ref, weights_ref, grads_ref, coded_ref):
    sources, _, sub, dh = recv_ref.shape
    ff = grads_ref.shape[-1]
    units = pl.ds(start, ff)
    gate_up = jnp.concatenate([weights_ref[0, :, units], weights_ref[2, :, units]], axis=1).astype(BF16)
    down = weights_ref[1, :, units].astype(BF16)
    for i in range(0, sources, chunk):
        rows = pl.ds(i, chunk)
        keys = recv_ref[rows, 0].reshape(chunk * sub, dh)
        values = recv_ref[rows, 1].reshape(chunk * sub, dh)
        pre = dot(keys, gate_up)
        gate, up = pre[:, :ff], pre[:, ff:]
        back = dot(values, down)
        sig = sigmoid(gate)
        act = gate * sig
        hidden = (act * up).astype(BF16)
        gate_grad = (back * up * (sig + act * (1.0 - sig))).astype(BF16)
        up_grad = (back * act).astype(BF16)
        sums = dot(keys.T, jnp.concatenate([gate_grad, up_grad], axis=1))
        sums = (sums[:, :ff], dot(values.T, hidden), sums[:, ff:])
        for m, value in enumerate(sums):
            grads_ref[m] = value if i == 0 else grads_ref[m] + value
    encode(grads_ref, coded_ref)


def encode(grads_ref, coded_ref):
    kinds, dh, ff = grads_ref.shape
    powers = []
    for m in range(kinds):
        for c in range(ff // LANES):
            block = grads_ref[m, :, c * LANES : (c + 1) * LANES]
            top = jnp.max(jnp.abs(block), axis=0, keepdims=True)
            power = jnp.floor(jnp.log2(jnp.maximum(top, 1e-30))) - 14.0
            code = jnp.clip(jnp.round(block * jnp.exp2(-power)), -32767.0, 32767.0)
            coded_ref[pl.ds(len(powers) * dh, dh)] = code.astype(jnp.int32).astype(jnp.int16)
            powers.append(power)
    rest = coded_ref.shape[0] - len(powers) * dh
    powers += [jnp.zeros_like(powers[0])] * (rest - len(powers))
    power = jnp.concatenate(powers, axis=0)
    coded_ref[pl.ds(coded_ref.shape[0] - rest, rest)] = power.astype(jnp.int32).astype(jnp.int16)


def decode(coded_ref, m, dh, ff):
    width = ff // LANES
    rest = code_rows(KINDS * width)
    power = coded_ref[pl.ds(coded_ref.shape[0] - rest, rest)].astype(jnp.int32).astype(F32)
    blocks = []
    for c in range(width):
        i = m * width + c
        code = coded_ref[pl.ds(i * dh, dh)].astype(jnp.int32).astype(F32)
        blocks.append(code * jnp.exp2(power[i : i + 1]))
    return jnp.concatenate(blocks, axis=1)


def code_rows(columns):
    return -(-columns // 16) * 16


def product(a, b):
    (ah, al), (bh, bl) = a, b
    return dot(jnp.concatenate([ah, al], axis=1), jnp.concatenate([bh, bh], axis=0)) + dot(ah, bl)


def newton_schulz(iterates, iters):
    for _ in range(iters):
        split = [halves(x) for x in iterates]
        gram = []
        for high, low in split:
            both = dot(high, jnp.concatenate([high, low], axis=0), NT)
            size = high.shape[0]
            cross = both[:, size:]
            gram.append(both[:, :size] + (cross + cross.T))
        gram_split = [halves(a) for a in gram]
        square = []
        for high, low in gram_split:
            wide = jnp.concatenate([high, low], axis=1)
            under = jnp.concatenate([high, jnp.zeros_like(high)], axis=1)
            both = dot(wide, jnp.concatenate([wide, under], axis=0))
            size = high.shape[0]
            square.append(both[:, :size] + both[:, size:])
        poly = [halves(COEF_B * a + COEF_C * b) for a, b in zip(gram, square)]
        iterates = [COEF_A * x + product(p, s) for x, p, s in zip(iterates, poly, split)]
    return iterates


def update_kernel(iters, coded, slot_ref, rate_ref, *refs):
    weights_ref, new_ref = refs[-2:]
    kinds, dh, ff = weights_ref.shape
    rate = rate_ref[slot_ref[0]]
    partials, others = refs[:-2], ()
    if coded:
        partials, others = refs[: len(refs) // 2 - 1], refs[len(refs) // 2 - 1 : -2]
    iterates = []
    for m in range(kinds):
        blocks = [partial[m] for partial in partials]
        if coded:
            blocks = [
                block + decode(other, m, dh, block.shape[-1])
                for block, other in zip(blocks, others)
            ]
        grad = jnp.concatenate(blocks, axis=1)
        iterates.append(grad * lax.rsqrt(jnp.sum(grad * grad) + 1e-06))
    iterates = newton_schulz(iterates, iters)
    for m in range(kinds):
        old = weights_ref[m]
        new = old + rate * iterates[m]
        old_norm = jnp.sqrt(jnp.sum(old * old, axis=0, keepdims=True) + 1e-06)
        new_norm = jnp.sqrt(jnp.sum(new * new, axis=0, keepdims=True) + 1e-06)
        new_ref[m] = (new * (old_norm / new_norm)).astype(BF16)


def read_kernel(chunk, new_ref, query_ref, read_ref):
    sources, sub, dh = query_ref.shape
    ff = new_ref.shape[-1]
    gate_up = jnp.concatenate([new_ref[0], new_ref[2]], axis=1)
    down = new_ref[1]

    def step(i, _):
        rows = pl.ds(i * chunk, chunk)
        pre = dot(query_ref[rows].reshape(chunk * sub, dh), gate_up)
        gate, up = pre[:, :ff], pre[:, ff:]
        hidden = (gate * sigmoid(gate) * up).astype(BF16)
        read = dot(hidden, down, NT).astype(BF16)
        read_ref[rows] = read.reshape(chunk, sub, dh)
        return 0

    lax.fori_loop(0, sources // chunk, step, 0)


def flat_heads(read_ref):
    return jnp.concatenate([read_ref[i] for i in range(read_ref.shape[0])], axis=1)


def project_own_kernel(column_ref, read_ref, weight_ref, sum_ref, *refs):
    rest_refs, (own_ref, sems) = refs[:-2], refs[-2:]
    depth, columns = own_ref.shape
    size = weight_ref.shape[0] // depth
    copies = []
    for s, target in enumerate((own_ref, *rest_refs)):
        rows = pl.ds(pl.multiple_of(lax.rem(column_ref[0] + size - s, size) * depth, depth), depth)
        copies.append(pltpu.make_async_copy(weight_ref.at[rows], target, sems.at[s]))
        copies[-1].start()
    copies[0].wait()
    sum_ref[...] = dot(flat_heads(read_ref), own_ref[...])
    for copy in copies[1:]:
        copy.wait()


def project_rest_kernel(sum_ref, *refs):
    reads, weights, out_ref = refs[: len(refs) // 2], refs[len(refs) // 2 : -1], refs[-1]
    value = sum_ref[...]
    for read, weight in zip(reads, weights):
        value = value + dot(flat_heads(read), weight[...])
    out_ref[...] = (value * sigmoid(value)).astype(BF16)


def call(kernel, out_shape, args, scalars=0, flops=None, limit=12, hbm=(), scratch=()):
    specs = [pl.BlockSpec(memory_space=pltpu.SMEM)] * scalars
    specs += [
        pl.BlockSpec(memory_space=pl.ANY if i in hbm else pltpu.VMEM)
        for i in range(scalars, len(args))
    ]
    cost = None
    if flops is not None:
        cost = pl.CostEstimate(flops=flops, bytes_accessed=2**20, transcendentals=0)
    return pl.pallas_call(
        kernel,
        out_shape=out_shape,
        in_specs=specs,
        out_specs=jax.tree.map(
            lambda _: pl.BlockSpec(memory_space=pl.ANY if -1 in hbm else pltpu.VMEM), out_shape
        ),
        scratch_shapes=list(scratch),
        compiler_params=pltpu.CompilerParams(vmem_limit_bytes=limit * 2**20),
        cost_estimate=cost,
    )(*args)


def on_device(tok_size, head_size, keys, values, queries, fast_weights, step_size, edit_mask, out_proj):
    tokens = keys.shape[0]
    kinds, heads, dh, ff = fast_weights.shape
    column = lax.axis_index("head")
    place = lax.axis_index("tok")
    count = tok_size // heads
    struct = jax.ShapeDtypeStruct
    both = ("tok", "head")

    quarter = tok_size // 4
    mixed = count == 2 and quarter * 4 == tok_size and head_size % 2 == 0
    slot = place % heads
    groups, turn = [], []
    for h in range(head_size):
        if mixed and h % 2 == 1:
            order = [q * quarter + i for q in (0, 2, 1, 3) for i in range(quarter)]
            partners = [t + quarter if t // quarter % 2 == 0 else t - quarter for t in range(tok_size)]
        else:
            order = list(range(tok_size))
            partners = [(t + heads) % tok_size for t in range(tok_size)]
        for g in range(count):
            groups.append([t * head_size + h for t in order[g * heads : (g + 1) * heads]])
        turn += [(t * head_size + h, partners[t] * head_size + h) for t in range(tok_size)]
    if mixed:
        other = place % quarter + quarter * (place // (2 * quarter))
        slot = jnp.where(column % 2 == 1, other, slot)

    def shuffle(x):
        return lax.all_to_all(x, both, 0, 0, tiled=True, axis_index_groups=groups)

    pairs = call(
        pack_kernel,
        struct((heads, 2, tokens, dh), BF16),
        (edit_mask[None], keys, values),
        hbm=(-1, 0, 1, 2),
        limit=60,
        scratch=[
            pltpu.VMEM((heads, 2, tokens, dh), BF16),
            pltpu.VMEM((1, *edit_mask.shape), edit_mask.dtype),
            pltpu.SemaphoreType.DMA((heads, 2)),
            pltpu.SemaphoreType.DMA((heads, 2)),
            pltpu.SemaphoreType.DMA,
        ],
    )
    received = shuffle(pairs)
    weights = lax.dynamic_index_in_dim(fast_weights, slot, 1, keepdims=False)
    chunk = max(c for c in (1, 2, 4) if heads % c == 0)
    split = 2 if ff % (2 * LANES) == 0 else 1
    width = ff // split
    partials, coded = [], []
    for start in range(0, ff, width):
        rows = kinds * dh * width // LANES + code_rows(kinds * width // LANES)
        partial, code = call(
            functools.partial(gradient_kernel, max(1, chunk // 2), start),
            (struct((kinds, dh, width), F32), struct((rows, LANES), jnp.int16)),
            (received, weights),
            flops=2**32,
            limit=16,
        )
        partials.append(partial)
        code, received = lax.optimization_barrier((code, received))
        coded.append(code)

    coded[-1], queries = lax.optimization_barrier((coded[-1], queries))
    packed = queries.reshape(tokens, heads, dh).transpose(1, 0, 2)
    if count == 2:
        arrived = [lax.ppermute(code, both, turn) for code in coded]
        parts = (*partials, *arrived)
    else:
        same = [[g * heads + i for g in range(count)] for i in range(heads)]
        parts = lax.psum(tuple(partials), "tok", axis_index_groups=same)
    asked = shuffle(packed)
    new = call(
        functools.partial(update_kernel, ITERS, count == 2),
        struct((kinds, dh, ff), BF16),
        (slot.reshape(1), step_size, *parts, weights),
        scalars=2,
        flops=2**33,
    )
    read = call(
        functools.partial(read_kernel, chunk), struct((heads, tokens, dh), BF16), (new, asked), limit=16
    )

    reads = shuffle(read)
    pieces = [
        lax.ppermute(reads, "head", [(i, (i + s) % head_size) for i in range(head_size)])
        for s in range(1, head_size)
    ]
    columns = out_proj.shape[1]
    depth = heads * dh
    own, *rest = call(
        project_own_kernel,
        (
            struct((tokens, columns), F32),
            *[struct((depth, columns), BF16) for _ in range(1, head_size)],
        ),
        (column.reshape(1), reads, out_proj),
        scalars=1,
        hbm=(2,),
        limit=49,
        scratch=[pltpu.VMEM((depth, columns), BF16), pltpu.SemaphoreType.DMA((head_size,))],
    )
    return call(
        project_rest_kernel, struct((tokens, columns), BF16), (own, *pieces, *rest)
    )


def solution(mesh):
    sizes = dict(mesh.shape)
    in_specs = (
        P("tok", "head"),
        P("tok", "head"),
        P("tok", "head"),
        P(None, "head", None, None),
        P("head"),
        P("tok"),
        P(None, "head"),
    )
    return jax.shard_map(
        functools.partial(on_device, sizes["tok"], sizes["head"]),
        mesh=mesh,
        in_specs=in_specs,
        out_specs=P("tok", "head"),
        check_vma=False,
    )
```

```python
import functools

import jax
import jax.numpy as jnp
from jax import lax
from jax.experimental import pallas as pl
from jax.experimental.pallas import tpu as pltpu
from jax.sharding import PartitionSpec as P

ITERS = 5
COEF_A = 3.4445
COEF_B = -4.775
COEF_C = 2.0315
BF16 = jnp.bfloat16
F32 = jnp.float32
LANES = 128
KINDS = 3
NN = (((1,), (0,)), ((), ()))
NT = (((1,), (1,)), ((), ()))
TN = (((0,), (0,)), ((), ()))


def dot(a, b, dims=NN):
    return lax.dot_general(a, b, dims, preferred_element_type=F32)


def halves(x):
    high = x.astype(BF16)
    return high, (x - high.astype(F32)).astype(BF16)


def sigmoid(x):
    return 0.5 + 0.5 * jnp.tanh(0.5 * x)


def pack_kernel(mask_ref, keys_ref, values_ref, pairs_ref, kept_ref, mask_kept, in_sem, out_sem, mask_sem):
    heads, _, tokens, dh = pairs_ref.shape
    blocks = mask_ref.shape[1]
    length = tokens // blocks
    sources = (keys_ref, values_ref)
    mask_copy = pltpu.make_async_copy(mask_ref, mask_kept, mask_sem)
    mask_copy.start()
    loads, stores = [], []
    for i in range(heads):
        for p in range(2):
            loads.append(
                pltpu.make_async_copy(
                    sources[p].at[:, pl.ds(i * dh, dh)], kept_ref.at[i, p], in_sem.at[i, p]
                )
            )
            stores.append(
                pltpu.make_async_copy(kept_ref.at[i, p], pairs_ref.at[i, p], out_sem.at[i, p])
            )
    for load in loads:
        load.start()
    mask_copy.wait()
    for i in range(heads):
        for p in range(2):
            loads[2 * i + p].wait()
            if p == 1:
                for b in range(blocks):
                    rows = pl.ds(b * length, length)
                    kept = kept_ref[i, 1, rows].astype(F32) * mask_kept[:, b : b + 1].astype(F32)
                    kept_ref[i, 1, rows] = kept.astype(BF16)
            stores[2 * i + p].start()
    for store in stores:
        store.wait()


def gradient_kernel(chunk, start, recv_ref, weights_ref, out_ref, *scratch):
    sources, _, sub, dh = recv_ref.shape
    grads_ref = scratch[0] if scratch else out_ref
    ff = grads_ref.shape[-1]
    units = pl.ds(start, ff)
    gate_up = jnp.concatenate([weights_ref[0, :, units], weights_ref[2, :, units]], axis=1).astype(BF16)
    down = weights_ref[1, :, units].astype(BF16)
    for i in range(0, sources, chunk):
        rows = pl.ds(i, chunk)
        keys = recv_ref[rows, 0].reshape(chunk * sub, dh)
        values = recv_ref[rows, 1].reshape(chunk * sub, dh)
        pre = dot(keys, gate_up)
        gate, up = pre[:, :ff], pre[:, ff:]
        back = dot(values, down)
        sig = sigmoid(gate)
        act = gate * sig
        hidden = (act * up).astype(BF16)
        gate_grad = (back * up * (sig + act * (1.0 - sig))).astype(BF16)
        up_grad = (back * act).astype(BF16)
        sums = dot(keys.T, jnp.concatenate([gate_grad, up_grad], axis=1))
        sums = (sums[:, :ff], dot(values.T, hidden), sums[:, ff:])
        for m, value in enumerate(sums):
            grads_ref[m] = value if i == 0 else grads_ref[m] + value
    if scratch:
        encode(grads_ref, out_ref)


def encode(grads_ref, coded_ref):
    kinds, dh, ff = grads_ref.shape
    powers = []
    for m in range(kinds):
        for c in range(ff // LANES):
            block = grads_ref[m, :, c * LANES : (c + 1) * LANES]
            top = jnp.max(jnp.abs(block), axis=0, keepdims=True)
            power = jnp.floor(jnp.log2(jnp.maximum(top, 1e-30))) - 14.0
            code = jnp.clip(jnp.round(block * jnp.exp2(-power)), -32767.0, 32767.0)
            coded_ref[pl.ds(len(powers) * dh, dh)] = code.astype(jnp.int32).astype(jnp.int16)
            powers.append(power)
    rest = coded_ref.shape[0] - len(powers) * dh
    powers += [jnp.zeros_like(powers[0])] * (rest - len(powers))
    power = jnp.concatenate(powers, axis=0)
    coded_ref[pl.ds(coded_ref.shape[0] - rest, rest)] = power.astype(jnp.int32).astype(jnp.int16)


def decode(coded_ref, m, dh, ff):
    width = ff // LANES
    rest = code_rows(KINDS * width)
    power = coded_ref[pl.ds(coded_ref.shape[0] - rest, rest)].astype(jnp.int32).astype(F32)
    blocks = []
    for c in range(width):
        i = m * width + c
        code = coded_ref[pl.ds(i * dh, dh)].astype(jnp.int32).astype(F32)
        blocks.append(code * jnp.exp2(power[i : i + 1]))
    return jnp.concatenate(blocks, axis=1)


def code_rows(columns):
    return -(-columns // 16) * 16


def square_product(a, b):
    (ah, al), (bh, bl) = a, b
    size = bh.shape[1]
    wide = jnp.concatenate([bh, bl], axis=1)
    both = dot(jnp.concatenate([ah, al], axis=1), jnp.concatenate([wide, wide], axis=0))
    return both[:, :size] + both[:, size:]


def product(a, b):
    (ah, al), (bh, bl) = a, b
    return dot(jnp.concatenate([ah, al], axis=1), jnp.concatenate([bh, bh], axis=0)) + dot(ah, bl)


def gram(x):
    high, low = x
    size = high.shape[0]
    both = dot(high, jnp.concatenate([high, low], axis=0), NT)
    cross = both[:, size:]
    return both[:, :size] + (cross + cross.T)


def newton_schulz(grads, iters):
    size = grads[0].shape[0]
    lines = lax.broadcasted_iota(jnp.int32, (size, size), 0)
    diagonal = lines == lax.broadcasted_iota(jnp.int32, (size, size), 1)
    split = [halves(x) for x in grads]
    grams = [gram(x) for x in split]
    scales = [
        1.0 / (jnp.sum(jnp.where(diagonal, a, 0.0), axis=(0, 1), keepdims=True) + 1e-06)
        for a in grams
    ]
    grams = [a * scale for a, scale in zip(grams, scales)]
    parts = [halves(a) for a in grams]
    polys = [halves(COEF_B * a + COEF_C * square_product(p, p)) for a, p in zip(grams, parts)]
    iterates = [
        (COEF_A * x + product(p, s)) * jnp.sqrt(scale)
        for x, p, s, scale in zip(grads, polys, split, scales)
    ]
    split = [halves(x) for x in iterates]
    grams = [gram(x) for x in split]
    steps = None
    for left in range(iters - 2, -1, -1):
        parts = [halves(a) for a in grams]
        polys = [
            halves(jnp.where(diagonal, COEF_A, 0.0) + (COEF_B * a + COEF_C * square_product(p, p)))
            for a, p in zip(grams, parts)
        ]
        if left > 0:
            inner = [halves(square_product(p, a)) for p, a in zip(polys, parts)]
            grams = [square_product(a, p) for a, p in zip(inner, polys)]
            if steps is None:
                steps = polys
            else:
                steps = [halves(square_product(p, q)) for p, q in zip(polys, steps)]
        if left == 1:
            split = [halves(product(q, s)) for q, s in zip(steps, split)]
    return [product(p, s) for p, s in zip(polys, split)]


def update_kernel(iters, coded, slot_ref, rate_ref, *refs):
    parts, (weights_ref, new_ref) = refs[:-2], refs[-2:]
    kinds, dh, ff = weights_ref.shape
    rate = rate_ref[slot_ref[0]]
    iterates = []
    for m in range(kinds):
        if coded:
            width = ff // (len(parts) // 2)
            blocks = [
                decode(own, m, dh, width) + decode(other, m, dh, width)
                for own, other in zip(parts[::2], parts[1::2])
            ]
        else:
            blocks = [part[m] for part in parts]
        iterates.append(jnp.concatenate(blocks, axis=1))
    iterates = newton_schulz(iterates, iters)
    for m in range(kinds):
        old = weights_ref[m]
        new = old + rate * iterates[m]
        old_norm = jnp.sqrt(jnp.sum(old * old, axis=0, keepdims=True) + 1e-06)
        new_norm = jnp.sqrt(jnp.sum(new * new, axis=0, keepdims=True) + 1e-06)
        new_ref[m] = (new * (old_norm / new_norm)).astype(BF16)


def merge_kernel(mine_ref, theirs_ref, both_ref):
    both_ref[:, 0] = mine_ref[...]
    both_ref[:, 1] = theirs_ref[...]


def read_kernel(chunk, side_ref, new_ref, query_ref, read_ref):
    half, sides, sub, dh = query_ref.shape
    ff = new_ref.shape[-1]
    gate_up = jnp.concatenate([new_ref[0], new_ref[2]], axis=1)
    down = new_ref[1]

    def step(i, _):
        rows = pl.ds(i * chunk, chunk)
        pre = dot(query_ref[rows].reshape(chunk * sides * sub, dh), gate_up)
        gate, up = pre[:, :ff], pre[:, ff:]
        hidden = (gate * sigmoid(gate) * up).astype(BF16)
        read = dot(hidden, down, NT).astype(BF16).reshape(chunk, sides, sub, dh)
        for p in range(sides):
            at = (side_ref[0] if p == 0 else 1 - side_ref[0]) * half + i * chunk
            read_ref[pl.ds(at, chunk)] = read[:, p]
        return 0

    lax.fori_loop(0, half // chunk, step, 0)


def flat_heads(read_ref):
    return jnp.concatenate([read_ref[i] for i in range(read_ref.shape[0])], axis=1)


def project_own_kernel(column_ref, read_ref, weight_ref, sum_ref, *refs):
    rest_refs, (own_ref, sems) = refs[:-2], refs[-2:]
    depth, columns = own_ref.shape
    size = weight_ref.shape[0] // depth
    copies = []
    for s, target in enumerate((own_ref, *rest_refs)):
        rows = pl.ds(pl.multiple_of(lax.rem(column_ref[0] + size - s, size) * depth, depth), depth)
        copies.append(pltpu.make_async_copy(weight_ref.at[rows], target, sems.at[s]))
        copies[-1].start()
    copies[0].wait()
    sum_ref[...] = dot(flat_heads(read_ref), own_ref[...])
    for copy in copies[1:]:
        copy.wait()


def project_rest_kernel(sum_ref, *refs):
    reads, weights, out_ref = refs[: len(refs) // 2], refs[len(refs) // 2 : -1], refs[-1]
    value = sum_ref[...]
    for read, weight in zip(reads, weights):
        value = value + dot(flat_heads(read), weight[...])
    out_ref[...] = (value * sigmoid(value)).astype(BF16)


def call(kernel, out_shape, args, scalars=0, flops=None, limit=12, hbm=(), scratch=()):
    specs = [pl.BlockSpec(memory_space=pltpu.SMEM)] * scalars
    specs += [
        pl.BlockSpec(memory_space=pl.ANY if i in hbm else pltpu.VMEM)
        for i in range(scalars, len(args))
    ]
    cost = None
    if flops is not None:
        cost = pl.CostEstimate(flops=flops, bytes_accessed=2**20, transcendentals=0)
    return pl.pallas_call(
        kernel,
        out_shape=out_shape,
        in_specs=specs,
        out_specs=jax.tree.map(
            lambda _: pl.BlockSpec(memory_space=pl.ANY if -1 in hbm else pltpu.VMEM), out_shape
        ),
        scratch_shapes=list(scratch),
        compiler_params=pltpu.CompilerParams(vmem_limit_bytes=limit * 2**20),
        cost_estimate=cost,
    )(*args)


def on_device(tok_size, head_size, keys, values, queries, fast_weights, step_size, edit_mask, out_proj):
    tokens = keys.shape[0]
    kinds, heads, dh, ff = fast_weights.shape
    column = lax.axis_index("head")
    place = lax.axis_index("tok")
    count = tok_size // heads
    struct = jax.ShapeDtypeStruct
    both = ("tok", "head")

    quarter = tok_size // 4
    mixed = count == 2 and quarter * 4 == tok_size and head_size % 2 == 0
    slot = place % heads
    groups, turn = [], []
    for h in range(head_size):
        if mixed and h % 2 == 1:
            order = [q * quarter + i for q in (0, 2, 1, 3) for i in range(quarter)]
            partners = [t + quarter if t // quarter % 2 == 0 else t - quarter for t in range(tok_size)]
        else:
            order = list(range(tok_size))
            partners = [(t + heads) % tok_size for t in range(tok_size)]
        for g in range(count):
            groups.append([t * head_size + h for t in order[g * heads : (g + 1) * heads]])
        turn += [(t * head_size + h, partners[t] * head_size + h) for t in range(tok_size)]
    if mixed:
        other = place % quarter + quarter * (place // (2 * quarter))
        slot = jnp.where(column % 2 == 1, other, slot)
    turned = heads // 2
    groups = [g[turned:] + g[:turned] for g in groups]
    slot = (slot + heads - turned) % heads

    def shuffle(x):
        return lax.all_to_all(x, both, 0, 0, tiled=True, axis_index_groups=groups)

    pairs = call(
        pack_kernel,
        struct((heads, 2, tokens, dh), BF16),
        (edit_mask[None], keys, values),
        hbm=(-1, 0, 1, 2),
        limit=60,
        scratch=[
            pltpu.VMEM((heads, 2, tokens, dh), BF16),
            pltpu.VMEM((1, *edit_mask.shape), edit_mask.dtype),
            pltpu.SemaphoreType.DMA((heads, 2)),
            pltpu.SemaphoreType.DMA((heads, 2)),
            pltpu.SemaphoreType.DMA,
        ],
    )
    received = shuffle(pairs)
    packed = queries.reshape(tokens, heads, dh).transpose(1, 0, 2)
    half = max(1, heads // 2)
    side = slot // half
    halves_of = [g[i : i + half] for g in groups for i in range(0, heads, half)]
    across = [(g[i], g[(i + half) % heads]) for g in groups for i in range(heads)]
    theirs = lax.dynamic_slice_in_dim(packed, (1 - side) * half, half, 0)
    theirs = lax.ppermute(theirs, both, across)
    mine = lax.dynamic_slice_in_dim(packed, side * half, half, 0)
    asked = call(merge_kernel, struct((half, 2, tokens, dh), BF16), (mine, theirs))
    weights = lax.dynamic_index_in_dim(fast_weights, slot, 1, keepdims=False)
    chunk = max(c for c in (1, 2, 4) if heads % c == 0)
    split = 2 if ff % (2 * LANES) == 0 else 1
    width = ff // split
    coded = count == 2
    partials = []
    for start in range(0, ff, width):
        sums = struct((kinds, dh, width), F32)
        rows = kinds * dh * width // LANES + code_rows(kinds * width // LANES)
        partial = call(
            functools.partial(gradient_kernel, max(1, chunk // 2), start),
            struct((rows, LANES), jnp.int16) if coded else sums,
            (received, weights),
            flops=2**32,
            limit=16,
            scratch=[pltpu.VMEM(sums.shape, F32)] if coded else [],
        )
        partials.append(partial)

    asked = lax.all_to_all(asked, both, 0, 0, tiled=True, axis_index_groups=halves_of)
    if coded:
        parts = [x for code in partials for x in (code, lax.ppermute(code, both, turn))]
    else:
        same = [[g * heads + i for g in range(count)] for i in range(heads)]
        parts = lax.psum(tuple(partials), "tok", axis_index_groups=same)
    new = call(
        functools.partial(update_kernel, ITERS, coded),
        struct((kinds, dh, ff), BF16),
        (slot.reshape(1), step_size, *parts, weights),
        scalars=2,
        flops=2**33,
    )
    read = call(
        functools.partial(read_kernel, max(1, chunk // 2)),
        struct((heads, tokens, dh), BF16),
        (side.reshape(1), new, asked),
        scalars=1,
        limit=16,
    )

    reads = shuffle(read)
    pieces = [
        lax.ppermute(reads, "head", [(i, (i + s) % head_size) for i in range(head_size)])
        for s in range(1, head_size)
    ]
    columns = out_proj.shape[1]
    depth = heads * dh
    own, *rest = call(
        project_own_kernel,
        (
            struct((tokens, columns), F32),
            *[struct((depth, columns), BF16) for _ in range(1, head_size)],
        ),
        (column.reshape(1), reads, out_proj),
        scalars=1,
        hbm=(2,),
        limit=49,
        scratch=[pltpu.VMEM((depth, columns), BF16), pltpu.SemaphoreType.DMA((head_size,))],
    )
    return call(
        project_rest_kernel, struct((tokens, columns), BF16), (own, *pieces, *rest)
    )


def solution(mesh):
    sizes = dict(mesh.shape)
    in_specs = (
        P("tok", "head"),
        P("tok", "head"),
        P("tok", "head"),
        P(None, "head", None, None),
        P("head"),
        P("tok"),
        P(None, "head"),
    )
    return jax.shard_map(
        functools.partial(on_device, sizes["tok"], sizes["head"]),
        mesh=mesh,
        in_specs=in_specs,
        out_specs=P("tok", "head"),
        check_vma=False,
    )
```

```python
import functools

import jax
import jax.numpy as jnp
from jax import lax
from jax.experimental import pallas as pl
from jax.experimental.pallas import tpu as pltpu
from jax.sharding import PartitionSpec as P

ITERS = 5
COEF_A = 3.4445
COEF_B = -4.775
COEF_C = 2.0315
BF16 = jnp.bfloat16
F32 = jnp.float32
LANES = 128
KINDS = 3
NN = (((1,), (0,)), ((), ()))
NT = (((1,), (1,)), ((), ()))
TN = (((0,), (0,)), ((), ()))


def dot(a, b, dims=NN):
    return lax.dot_general(a, b, dims, preferred_element_type=F32)


def halves(x):
    high = x.astype(BF16)
    return high, (x - high.astype(F32)).astype(BF16)


def sigmoid(x):
    return 0.5 + 0.5 * jnp.tanh(0.5 * x)


def pack_kernel(mask_ref, keys_ref, values_ref, pairs_ref, kept_ref, mask_kept, in_sem, out_sem, mask_sem):
    heads, _, tokens, dh = pairs_ref.shape
    blocks = mask_ref.shape[1]
    length = tokens // blocks
    sources = (keys_ref, values_ref)
    mask_copy = pltpu.make_async_copy(mask_ref, mask_kept, mask_sem)
    mask_copy.start()
    loads, stores = [], []
    for i in range(heads):
        for p in range(2):
            loads.append(
                pltpu.make_async_copy(
                    sources[p].at[:, pl.ds(i * dh, dh)], kept_ref.at[i, p], in_sem.at[i, p]
                )
            )
            stores.append(
                pltpu.make_async_copy(kept_ref.at[i, p], pairs_ref.at[i, p], out_sem.at[i, p])
            )
    for load in loads:
        load.start()
    mask_copy.wait()
    for i in range(heads):
        for p in range(2):
            loads[2 * i + p].wait()
            if p == 1:
                for b in range(blocks):
                    rows = pl.ds(b * length, length)
                    kept = kept_ref[i, 1, rows].astype(F32) * mask_kept[:, b : b + 1].astype(F32)
                    kept_ref[i, 1, rows] = kept.astype(BF16)
            stores[2 * i + p].start()
    for store in stores:
        store.wait()


def gradient_kernel(chunk, start, recv_ref, weights_ref, out_ref, *scratch):
    sources, _, sub, dh = recv_ref.shape
    grads_ref = scratch[0] if scratch else out_ref
    ff = grads_ref.shape[-1]
    units = pl.ds(start, ff)
    gate_up = jnp.concatenate([weights_ref[0, :, units], weights_ref[2, :, units]], axis=1).astype(BF16)
    down = weights_ref[1, :, units].astype(BF16)
    for i in range(0, sources, chunk):
        rows = pl.ds(i, chunk)
        keys = recv_ref[rows, 0].reshape(chunk * sub, dh)
        values = recv_ref[rows, 1].reshape(chunk * sub, dh)
        pre = dot(keys, gate_up)
        gate, up = pre[:, :ff], pre[:, ff:]
        back = dot(values, down)
        sig = sigmoid(gate)
        act = gate * sig
        hidden = (act * up).astype(BF16)
        gate_grad = (back * up * (sig + act * (1.0 - sig))).astype(BF16)
        up_grad = (back * act).astype(BF16)
        sums = dot(keys.T, jnp.concatenate([gate_grad, up_grad], axis=1))
        sums = (sums[:, :ff], dot(values.T, hidden), sums[:, ff:])
        for m, value in enumerate(sums):
            grads_ref[m] = value if i == 0 else grads_ref[m] + value
    if scratch:
        encode(grads_ref, out_ref)


def encode(grads_ref, coded_ref):
    kinds, dh, ff = grads_ref.shape
    powers = []
    for m in range(kinds):
        for c in range(ff // LANES):
            block = grads_ref[m, :, c * LANES : (c + 1) * LANES]
            top = jnp.max(jnp.abs(block), axis=0, keepdims=True)
            power = jnp.floor(jnp.log2(jnp.maximum(top, 1e-30))) - 14.0
            code = jnp.clip(jnp.round(block * jnp.exp2(-power)), -32767.0, 32767.0)
            coded_ref[pl.ds(len(powers) * dh, dh)] = code.astype(jnp.int32).astype(jnp.int16)
            powers.append(power)
    rest = coded_ref.shape[0] - len(powers) * dh
    powers += [jnp.zeros_like(powers[0])] * (rest - len(powers))
    power = jnp.concatenate(powers, axis=0)
    coded_ref[pl.ds(coded_ref.shape[0] - rest, rest)] = power.astype(jnp.int32).astype(jnp.int16)


def decode(coded_ref, m, dh, ff):
    width = ff // LANES
    rest = code_rows(KINDS * width)
    power = coded_ref[pl.ds(coded_ref.shape[0] - rest, rest)].astype(jnp.int32).astype(F32)
    blocks = []
    for c in range(width):
        i = m * width + c
        code = coded_ref[pl.ds(i * dh, dh)].astype(jnp.int32).astype(F32)
        blocks.append(code * jnp.exp2(power[i : i + 1]))
    return jnp.concatenate(blocks, axis=1)


def code_rows(columns):
    return -(-columns // 16) * 16


def square_product(a, b):
    (ah, al), (bh, bl) = a, b
    size = bh.shape[1]
    wide = jnp.concatenate([bh, bl], axis=1)
    both = dot(jnp.concatenate([ah, al], axis=1), jnp.concatenate([wide, wide], axis=0))
    return both[:, :size] + both[:, size:]


def product(a, b):
    (ah, al), (bh, bl) = a, b
    return dot(jnp.concatenate([ah, al], axis=1), jnp.concatenate([bh, bh], axis=0)) + dot(ah, bl)


def gram(x):
    high, low = x
    size = high.shape[0]
    both = dot(high, jnp.concatenate([high, low], axis=0), NT)
    cross = both[:, size:]
    return both[:, :size] + (cross + cross.T)


def newton_schulz(grads, iters):
    size = grads[0].shape[0]
    lines = lax.broadcasted_iota(jnp.int32, (size, size), 0)
    diagonal = lines == lax.broadcasted_iota(jnp.int32, (size, size), 1)
    split = [halves(x) for x in grads]
    grams = [gram(x) for x in split]
    scales = [
        1.0 / (jnp.sum(jnp.where(diagonal, a, 0.0), axis=(0, 1), keepdims=True) + 1e-06)
        for a in grams
    ]
    grams = [a * scale for a, scale in zip(grams, scales)]
    parts = [halves(a) for a in grams]
    polys = [halves(COEF_B * a + COEF_C * square_product(p, p)) for a, p in zip(grams, parts)]
    iterates = [
        (COEF_A * x + product(p, s)) * jnp.sqrt(scale)
        for x, p, s, scale in zip(grads, polys, split, scales)
    ]
    split = [halves(x) for x in iterates]
    grams = [gram(x) for x in split]
    steps = None
    for left in range(iters - 2, -1, -1):
        parts = [halves(a) for a in grams]
        polys = [
            halves(jnp.where(diagonal, COEF_A, 0.0) + (COEF_B * a + COEF_C * square_product(p, p)))
            for a, p in zip(grams, parts)
        ]
        if left > 0:
            inner = [halves(square_product(p, a)) for p, a in zip(polys, parts)]
            grams = [square_product(a, p) for a, p in zip(inner, polys)]
            if steps is None:
                steps = polys
            else:
                steps = [halves(square_product(p, q)) for p, q in zip(polys, steps)]
        if left == 1:
            split = [halves(product(q, s)) for q, s in zip(steps, split)]
    return [product(p, s) for p, s in zip(polys, split)]


def update_kernel(iters, coded, slot_ref, rate_ref, *refs):
    parts, (weights_ref, new_ref) = refs[:-2], refs[-2:]
    kinds, dh, ff = weights_ref.shape
    rate = rate_ref[slot_ref[0]]
    iterates = []
    for m in range(kinds):
        if coded:
            width = ff // (len(parts) // 2)
            blocks = [
                decode(own, m, dh, width) + decode(other, m, dh, width)
                for own, other in zip(parts[::2], parts[1::2])
            ]
        else:
            blocks = [part[m] for part in parts]
        iterates.append(jnp.concatenate(blocks, axis=1))
    iterates = newton_schulz(iterates, iters)
    for m in range(kinds):
        old = weights_ref[m]
        new = old + rate * iterates[m]
        old_norm = jnp.sqrt(jnp.sum(old * old, axis=0, keepdims=True) + 1e-06)
        new_norm = jnp.sqrt(jnp.sum(new * new, axis=0, keepdims=True) + 1e-06)
        new_ref[m] = (new * (old_norm / new_norm)).astype(BF16)


def merge_kernel(mine_ref, theirs_ref, both_ref):
    both_ref[:, 0] = mine_ref[...]
    both_ref[:, 1] = theirs_ref[...]


def read_kernel(chunk, side_ref, new_ref, query_ref, read_ref):
    half, sides, sub, dh = query_ref.shape
    ff = new_ref.shape[-1]
    gate_up = jnp.concatenate([new_ref[0], new_ref[2]], axis=1)
    down = new_ref[1]

    for i in range(0, half, chunk):
        pre = dot(query_ref[pl.ds(i, chunk)].reshape(chunk * sides * sub, dh), gate_up)
        gate, up = pre[:, :ff], pre[:, ff:]
        hidden = (gate * sigmoid(gate) * up).astype(BF16)
        read = dot(hidden, down, NT).astype(BF16).reshape(chunk, sides, sub, dh)
        for c in range(chunk):
            read_ref[spot(side_ref[0], i + c, half)] = read[c, 0]
            if sides == 2:
                read_ref[spot(1 - side_ref[0], i + c, half)] = read[c, 1]


def spot(side, i, half):
    if half % 2 == 0:
        return (half // 2 - 1 - i // 2) * 4 + side * 2 + 1 - i % 2
    return side * half + half - 1 - i


def flat_heads(read_ref):
    heads = read_ref.shape[0]
    half = max(1, heads // 2)
    return jnp.concatenate([read_ref[spot(i // half, i % half, half)] for i in range(heads)], axis=1)


def project_own_kernel(column_ref, read_ref, weight_ref, sum_ref, *refs):
    rest_refs, (own_ref, sems) = refs[:-2], refs[-2:]
    depth, columns = own_ref.shape
    size = weight_ref.shape[0] // depth
    copies = []
    for s, target in enumerate((own_ref, *rest_refs)):
        rows = pl.ds(pl.multiple_of(lax.rem(column_ref[0] + size - s, size) * depth, depth), depth)
        copies.append(pltpu.make_async_copy(weight_ref.at[rows], target, sems.at[s]))
        copies[-1].start()
    copies[0].wait()
    sum_ref[...] = dot(flat_heads(read_ref), own_ref[...])
    for copy in copies[1:]:
        copy.wait()


def project_rest_kernel(sum_ref, *refs):
    reads, weights, out_ref = refs[: len(refs) // 2], refs[len(refs) // 2 : -1], refs[-1]
    value = sum_ref[...]
    for read, weight in zip(reads, weights):
        value = value + dot(flat_heads(read), weight[...])
    out_ref[...] = (value * sigmoid(value)).astype(BF16)


def call(kernel, out_shape, args, scalars=0, flops=None, limit=12, hbm=(), scratch=()):
    specs = [pl.BlockSpec(memory_space=pltpu.SMEM)] * scalars
    specs += [
        pl.BlockSpec(memory_space=pl.ANY if i in hbm else pltpu.VMEM)
        for i in range(scalars, len(args))
    ]
    cost = None
    if flops is not None:
        cost = pl.CostEstimate(flops=flops, bytes_accessed=2**20, transcendentals=0)
    return pl.pallas_call(
        kernel,
        out_shape=out_shape,
        in_specs=specs,
        out_specs=jax.tree.map(
            lambda _: pl.BlockSpec(memory_space=pl.ANY if -1 in hbm else pltpu.VMEM), out_shape
        ),
        scratch_shapes=list(scratch),
        compiler_params=pltpu.CompilerParams(vmem_limit_bytes=limit * 2**20),
        cost_estimate=cost,
    )(*args)


def on_device(tok_size, head_size, keys, values, queries, fast_weights, step_size, edit_mask, out_proj):
    tokens = keys.shape[0]
    kinds, heads, dh, ff = fast_weights.shape
    column = lax.axis_index("head")
    place = lax.axis_index("tok")
    count = tok_size // heads
    struct = jax.ShapeDtypeStruct
    both = ("tok", "head")

    quarter = tok_size // 4
    mixed = count == 2 and quarter * 4 == tok_size and head_size % 2 == 0
    slot = place % heads
    groups, turn = [], []
    for h in range(head_size):
        if mixed and h % 2 == 1:
            order = [q * quarter + i for q in (0, 2, 1, 3) for i in range(quarter)]
            partners = [t + quarter if t // quarter % 2 == 0 else t - quarter for t in range(tok_size)]
        else:
            order = list(range(tok_size))
            partners = [(t + heads) % tok_size for t in range(tok_size)]
        for g in range(count):
            groups.append([t * head_size + h for t in order[g * heads : (g + 1) * heads]])
        turn += [(t * head_size + h, partners[t] * head_size + h) for t in range(tok_size)]
    if mixed:
        other = place % quarter + quarter * (place // (2 * quarter))
        slot = jnp.where(column % 2 == 1, other, slot)
    turned = heads // 2
    groups = [g[turned:] + g[:turned] for g in groups]
    slot = (slot + heads - turned) % heads

    pairs = call(
        pack_kernel,
        struct((heads, 2, tokens, dh), BF16),
        (edit_mask[None], keys, values),
        hbm=(-1, 0, 1, 2),
        limit=60,
        scratch=[
            pltpu.VMEM((heads, 2, tokens, dh), BF16),
            pltpu.VMEM((1, *edit_mask.shape), edit_mask.dtype),
            pltpu.SemaphoreType.DMA((heads, 2)),
            pltpu.SemaphoreType.DMA((heads, 2)),
            pltpu.SemaphoreType.DMA,
        ],
    )
    received = lax.all_to_all(pairs, both, 0, 0, tiled=True, axis_index_groups=groups)
    packed = queries.reshape(tokens, heads, dh).transpose(1, 0, 2)
    half = max(1, heads // 2)
    side = slot // half
    halves_of = [g[i : i + half] for g in groups for i in range(0, heads, half)]
    across = [(g[i], g[(i + half) % heads]) for g in groups for i in range(heads)]
    theirs = lax.dynamic_slice_in_dim(packed, (1 - side) * half, half, 0)
    theirs = lax.ppermute(theirs, both, across)
    mine = lax.dynamic_slice_in_dim(packed, side * half, half, 0)
    asked = call(merge_kernel, struct((half, 2, tokens, dh), BF16), (mine, theirs))
    weights = lax.dynamic_index_in_dim(fast_weights, slot, 1, keepdims=False)
    chunk = max(c for c in (1, 2, 4) if heads % c == 0)
    split = 2 if ff % (2 * LANES) == 0 else 1
    width = ff // split
    coded = count == 2
    partials = []
    for start in range(0, ff, width):
        sums = struct((kinds, dh, width), F32)
        rows = kinds * dh * width // LANES + code_rows(kinds * width // LANES)
        partial = call(
            functools.partial(gradient_kernel, max(1, chunk // 2), start),
            struct((rows, LANES), jnp.int16) if coded else sums,
            (received, weights),
            flops=2**32,
            limit=16,
            scratch=[pltpu.VMEM(sums.shape, F32)] if coded else [],
        )
        partials.append(partial)

    asked = lax.all_to_all(asked, both, 0, 0, tiled=True, axis_index_groups=halves_of)
    if coded:
        parts = [x for code in partials for x in (code, lax.ppermute(code, both, turn))]
    else:
        same = [[g * heads + i for g in range(count)] for i in range(heads)]
        parts = lax.psum(tuple(partials), "tok", axis_index_groups=same)
    new = call(
        functools.partial(update_kernel, ITERS, coded),
        struct((kinds, dh, ff), BF16),
        (slot.reshape(1), step_size, *parts, weights),
        scalars=2,
        flops=2**33,
    )
    read = call(
        functools.partial(read_kernel, max(1, chunk // 2)),
        struct((heads, tokens, dh), BF16),
        (side.reshape(1), new, asked),
        scalars=1,
        limit=16,
    )

    places = sorted(range(heads), key=lambda i: spot(i // half, i % half, half))
    reads = lax.all_to_all(
        read, both, 0, 0, tiled=True, axis_index_groups=[[g[i] for i in places] for g in groups]
    )
    pieces = [
        lax.ppermute(reads, "head", [(i, (i + s) % head_size) for i in range(head_size)])
        for s in range(1, head_size)
    ]
    columns = out_proj.shape[1]
    depth = heads * dh
    own, *rest = call(
        project_own_kernel,
        (
            struct((tokens, columns), F32),
            *[struct((depth, columns), BF16) for _ in range(1, head_size)],
        ),
        (column.reshape(1), reads, out_proj),
        scalars=1,
        hbm=(2,),
        limit=49,
        scratch=[pltpu.VMEM((depth, columns), BF16), pltpu.SemaphoreType.DMA((head_size,))],
    )
    return call(
        project_rest_kernel, struct((tokens, columns), BF16), (own, *pieces, *rest)
    )


def solution(mesh):
    sizes = dict(mesh.shape)
    in_specs = (
        P("tok", "head"),
        P("tok", "head"),
        P("tok", "head"),
        P(None, "head", None, None),
        P("head"),
        P("tok"),
        P(None, "head"),
    )
    return jax.shard_map(
        functools.partial(on_device, sizes["tok"], sizes["head"]),
        mesh=mesh,
        in_specs=in_specs,
        out_specs=P("tok", "head"),
        check_vma=False,
    )
```

```python
import functools

import jax
import jax.numpy as jnp
from jax import lax
from jax.experimental import pallas as pl
from jax.experimental.pallas import tpu as pltpu
from jax.sharding import PartitionSpec as P

ITERS = 5
COEF_A = 3.4445
COEF_B = -4.775
COEF_C = 2.0315
BF16 = jnp.bfloat16
F32 = jnp.float32
LANES = 128
KINDS = 3
NN = (((1,), (0,)), ((), ()))
NT = (((1,), (1,)), ((), ()))
TN = (((0,), (0,)), ((), ()))


def dot(a, b, dims=NN):
    return lax.dot_general(a, b, dims, preferred_element_type=F32)


def halves(x):
    high = x.astype(BF16)
    return high, (x - high.astype(F32)).astype(BF16)


def sigmoid(x):
    return 0.5 + 0.5 * jnp.tanh(0.5 * x)


def pack_kernel(mask_ref, keys_ref, values_ref, pairs_ref, wide_ref, kept_ref, mask_kept, in_sem, out_sem, mask_sem):
    heads, _, tokens, dh = pairs_ref.shape
    blocks = mask_ref.shape[1]
    shares = in_sem.shape[1]
    length = tokens // shares
    sources = (keys_ref, values_ref)
    mask_copy = pltpu.make_async_copy(mask_ref, mask_kept, mask_sem)
    mask_copy.start()
    loads, stores = [], []
    for r in range(shares):
        rows = pl.ds(r * length, length)
        for p in range(2):
            loads.append(
                pltpu.make_async_copy(sources[p].at[rows], wide_ref.at[p, rows], in_sem.at[p, r])
            )
            loads[-1].start()
    mask_copy.wait()
    for r in range(shares):
        rows = pl.ds(r * length, length)
        for p in range(2):
            loads[2 * r + p].wait()
            for i in range(heads):
                columns = pl.ds(i * dh, dh)
                if p == 0:
                    kept_ref[i, p, rows] = wide_ref[p, rows, columns]
                    continue
                size = min(length, tokens // blocks)
                for start in range(r * length, (r + 1) * length, size):
                    some = pl.ds(start, size)
                    b = start // (tokens // blocks)
                    kept = wide_ref[p, some, columns].astype(F32) * mask_kept[:, b : b + 1].astype(F32)
                    kept_ref[i, p, some] = kept.astype(BF16)
            stores.append(
                pltpu.make_async_copy(
                    kept_ref.at[:, p, rows], pairs_ref.at[:, p, rows], out_sem.at[p, r]
                )
            )
            stores[-1].start()
    for store in stores:
        store.wait()


def gradient_kernel(chunk, start, recv_ref, weights_ref, out_ref, *scratch):
    sources, _, sub, dh = recv_ref.shape
    grads_ref = scratch[0] if scratch else out_ref
    ff = grads_ref.shape[-1]
    units = pl.ds(start, ff)
    gate_up = jnp.concatenate([weights_ref[0, :, units], weights_ref[2, :, units]], axis=1).astype(BF16)
    down = weights_ref[1, :, units].astype(BF16)
    for i in range(0, sources, chunk):
        rows = pl.ds(i, chunk)
        keys = recv_ref[rows, 0].reshape(chunk * sub, dh)
        values = recv_ref[rows, 1].reshape(chunk * sub, dh)
        pre = dot(keys, gate_up)
        gate, up = pre[:, :ff], pre[:, ff:]
        back = dot(values, down)
        sig = sigmoid(gate)
        act = gate * sig
        hidden = (act * up).astype(BF16)
        gate_grad = (back * up * (sig + act * (1.0 - sig))).astype(BF16)
        up_grad = (back * act).astype(BF16)
        sums = dot(keys.T, jnp.concatenate([gate_grad, up_grad], axis=1))
        sums = (sums[:, :ff], dot(values.T, hidden), sums[:, ff:])
        for m, value in enumerate(sums):
            grads_ref[m] = value if i == 0 else grads_ref[m] + value
    if scratch:
        encode(grads_ref, out_ref)


def encode(grads_ref, coded_ref):
    kinds, dh, ff = grads_ref.shape
    powers = []
    for m in range(kinds):
        for c in range(ff // LANES):
            block = grads_ref[m, :, c * LANES : (c + 1) * LANES]
            top = jnp.max(jnp.abs(block), axis=0, keepdims=True)
            power = jnp.floor(jnp.log2(jnp.maximum(top, 1e-30))) - 14.0
            code = jnp.clip(jnp.round(block * jnp.exp2(-power)), -32767.0, 32767.0)
            coded_ref[pl.ds(len(powers) * dh, dh)] = code.astype(jnp.int32).astype(jnp.int16)
            powers.append(power)
    rest = coded_ref.shape[0] - len(powers) * dh
    powers += [jnp.zeros_like(powers[0])] * (rest - len(powers))
    power = jnp.concatenate(powers, axis=0)
    coded_ref[pl.ds(coded_ref.shape[0] - rest, rest)] = power.astype(jnp.int32).astype(jnp.int16)


def decode(coded_ref, m, dh, ff):
    width = ff // LANES
    rest = code_rows(KINDS * width)
    power = coded_ref[pl.ds(coded_ref.shape[0] - rest, rest)].astype(jnp.int32).astype(F32)
    blocks = []
    for c in range(width):
        i = m * width + c
        code = coded_ref[pl.ds(i * dh, dh)].astype(jnp.int32).astype(F32)
        blocks.append(code * jnp.exp2(power[i : i + 1]))
    return jnp.concatenate(blocks, axis=1)


def code_rows(columns):
    return -(-columns // 16) * 16


def square_product(a, b):
    (ah, al), (bh, bl) = a, b
    size = bh.shape[1]
    wide = jnp.concatenate([bh, bl], axis=1)
    both = dot(jnp.concatenate([ah, al], axis=1), jnp.concatenate([wide, wide], axis=0))
    return both[:, :size] + both[:, size:]


def product(a, b):
    (ah, al), (bh, bl) = a, b
    return dot(jnp.concatenate([ah, al], axis=1), jnp.concatenate([bh, bh], axis=0)) + dot(ah, bl)


def gram(x):
    high, low = x
    size = high.shape[0]
    both = dot(high, jnp.concatenate([high, low], axis=0), NT)
    cross = both[:, size:]
    return both[:, :size] + (cross + cross.T)


def newton_schulz(grads, iters):
    size = grads[0].shape[0]
    lines = lax.broadcasted_iota(jnp.int32, (size, size), 0)
    diagonal = lines == lax.broadcasted_iota(jnp.int32, (size, size), 1)
    split = [halves(x) for x in grads]
    grams = [gram(x) for x in split]
    scales = [
        1.0 / (jnp.sum(jnp.where(diagonal, a, 0.0), axis=(0, 1), keepdims=True) + 1e-06)
        for a in grams
    ]
    grams = [a * scale for a, scale in zip(grams, scales)]
    parts = [halves(a) for a in grams]
    polys = [halves(COEF_B * a + COEF_C * square_product(p, p)) for a, p in zip(grams, parts)]
    iterates = [
        (COEF_A * x + product(p, s)) * jnp.sqrt(scale)
        for x, p, s, scale in zip(grads, polys, split, scales)
    ]
    split = [halves(x) for x in iterates]
    grams = [gram(x) for x in split]
    steps = None
    for left in range(iters - 2, -1, -1):
        parts = [halves(a) for a in grams]
        polys = [
            halves(jnp.where(diagonal, COEF_A, 0.0) + (COEF_B * a + COEF_C * square_product(p, p)))
            for a, p in zip(grams, parts)
        ]
        if left > 0:
            inner = [halves(square_product(p, a)) for p, a in zip(polys, parts)]
            grams = [square_product(a, p) for a, p in zip(inner, polys)]
            if steps is None:
                steps = polys
            else:
                steps = [halves(square_product(p, q)) for p, q in zip(polys, steps)]
        if left == 1:
            split = [halves(product(q, s)) for q, s in zip(steps, split)]
    return [product(p, s) for p, s in zip(polys, split)]


def update_kernel(iters, coded, slot_ref, rate_ref, *refs):
    parts, (weights_ref, new_ref) = refs[:-2], refs[-2:]
    kinds, dh, ff = weights_ref.shape
    rate = rate_ref[slot_ref[0]]
    iterates = []
    for m in range(kinds):
        if coded:
            width = ff // (len(parts) // 2)
            blocks = [
                decode(own, m, dh, width) + decode(other, m, dh, width)
                for own, other in zip(parts[::2], parts[1::2])
            ]
        else:
            blocks = [part[m] for part in parts]
        iterates.append(jnp.concatenate(blocks, axis=1))
    iterates = newton_schulz(iterates, iters)
    for m in range(kinds):
        old = weights_ref[m]
        new = old + rate * iterates[m]
        old_norm = jnp.sqrt(jnp.sum(old * old, axis=0, keepdims=True) + 1e-06)
        new_norm = jnp.sqrt(jnp.sum(new * new, axis=0, keepdims=True) + 1e-06)
        new_ref[m] = (new * (old_norm / new_norm)).astype(BF16)


def merge_kernel(mine_ref, theirs_ref, both_ref):
    both_ref[:, 0] = mine_ref[...]
    both_ref[:, 1] = theirs_ref[...]


def read_kernel(chunk, side_ref, new_ref, query_ref, read_ref):
    half, sides, sub, dh = query_ref.shape
    ff = new_ref.shape[-1]
    gate_up = jnp.concatenate([new_ref[0], new_ref[2]], axis=1)
    down = new_ref[1]

    for i in range(0, half, chunk):
        pre = dot(query_ref[pl.ds(i, chunk)].reshape(chunk * sides * sub, dh), gate_up)
        gate, up = pre[:, :ff], pre[:, ff:]
        hidden = (gate * sigmoid(gate) * up).astype(BF16)
        read = dot(hidden, down, NT).astype(BF16).reshape(chunk, sides, sub, dh)
        for c in range(chunk):
            read_ref[spot(side_ref[0], i + c, half)] = read[c, 0]
            if sides == 2:
                read_ref[spot(1 - side_ref[0], i + c, half)] = read[c, 1]


def spot(side, i, half):
    if half % 2 == 0:
        return (half // 2 - 1 - i // 2) * 4 + side * 2 + 1 - i % 2
    return side * half + half - 1 - i


def flat_heads(read_ref):
    heads = read_ref.shape[0]
    half = max(1, heads // 2)
    return jnp.concatenate([read_ref[spot(i // half, i % half, half)] for i in range(heads)], axis=1)


def project_own_kernel(column_ref, read_ref, weight_ref, sum_ref, *refs):
    rest_refs, (own_ref, sems) = refs[:-2], refs[-2:]
    depth, columns = own_ref.shape
    size = weight_ref.shape[0] // depth
    copies = []
    for s, target in enumerate((own_ref, *rest_refs)):
        rows = pl.ds(pl.multiple_of(lax.rem(column_ref[0] + size - s, size) * depth, depth), depth)
        copies.append(pltpu.make_async_copy(weight_ref.at[rows], target, sems.at[s]))
        copies[-1].start()
    copies[0].wait()
    sum_ref[...] = dot(flat_heads(read_ref), own_ref[...])
    for copy in copies[1:]:
        copy.wait()


def project_rest_kernel(sum_ref, *refs):
    refs, (out_ref, held_ref, sems) = refs[:-3], refs[-3:]
    reads, weights = refs[: len(refs) // 2], refs[len(refs) // 2 :]
    flats = [flat_heads(read) for read in reads]
    shares = sems.shape[0]
    width = held_ref.shape[1] // shares
    copies = []
    for i in range(shares):
        columns = pl.ds(i * width, width)
        value = sum_ref[:, columns]
        for flat, weight in zip(flats, weights):
            value = value + dot(flat, weight[:, columns])
        held_ref[:, columns] = (value * sigmoid(value)).astype(BF16)
        copies.append(
            pltpu.make_async_copy(held_ref.at[:, columns], out_ref.at[:, columns], sems.at[i])
        )
        copies[-1].start()
    for copy in copies:
        copy.wait()


def call(kernel, out_shape, args, scalars=0, flops=None, limit=12, hbm=(), scratch=()):
    specs = [pl.BlockSpec(memory_space=pltpu.SMEM)] * scalars
    specs += [
        pl.BlockSpec(memory_space=pl.ANY if i in hbm else pltpu.VMEM)
        for i in range(scalars, len(args))
    ]
    cost = None
    if flops is not None:
        cost = pl.CostEstimate(flops=flops, bytes_accessed=2**20, transcendentals=0)
    return pl.pallas_call(
        kernel,
        out_shape=out_shape,
        in_specs=specs,
        out_specs=jax.tree.map(
            lambda _: pl.BlockSpec(memory_space=pl.ANY if -1 in hbm else pltpu.VMEM), out_shape
        ),
        scratch_shapes=list(scratch),
        compiler_params=pltpu.CompilerParams(vmem_limit_bytes=limit * 2**20),
        cost_estimate=cost,
    )(*args)


def on_device(tok_size, head_size, keys, values, queries, fast_weights, step_size, edit_mask, out_proj):
    tokens = keys.shape[0]
    kinds, heads, dh, ff = fast_weights.shape
    column = lax.axis_index("head")
    place = lax.axis_index("tok")
    count = tok_size // heads
    struct = jax.ShapeDtypeStruct
    both = ("tok", "head")

    quarter = tok_size // 4
    mixed = count == 2 and quarter * 4 == tok_size and head_size % 2 == 0
    slot = place % heads
    groups, turn = [], []
    for h in range(head_size):
        if mixed and h % 2 == 1:
            order = [q * quarter + i for q in (0, 2, 1, 3) for i in range(quarter)]
            partners = [t + quarter if t // quarter % 2 == 0 else t - quarter for t in range(tok_size)]
        else:
            order = list(range(tok_size))
            partners = [(t + heads) % tok_size for t in range(tok_size)]
        for g in range(count):
            groups.append([t * head_size + h for t in order[g * heads : (g + 1) * heads]])
        turn += [(t * head_size + h, partners[t] * head_size + h) for t in range(tok_size)]
    if mixed:
        other = place % quarter + quarter * (place // (2 * quarter))
        slot = jnp.where(column % 2 == 1, other, slot)
    turned = heads // 2
    groups = [g[turned:] + g[:turned] for g in groups]
    slot = (slot + heads - turned) % heads

    pairs = call(
        pack_kernel,
        struct((heads, 2, tokens, dh), BF16),
        (edit_mask[None], keys, values),
        hbm=(-1, 0, 1, 2),
        limit=60,
        scratch=[
            pltpu.VMEM((2, tokens, heads * dh), BF16),
            pltpu.VMEM((heads, 2, tokens, dh), BF16),
            pltpu.VMEM((1, *edit_mask.shape), edit_mask.dtype),
            pltpu.SemaphoreType.DMA((2, 2)),
            pltpu.SemaphoreType.DMA((2, 2)),
            pltpu.SemaphoreType.DMA,
        ],
    )
    received = lax.all_to_all(pairs, both, 0, 0, tiled=True, axis_index_groups=groups)
    packed = queries.reshape(tokens, heads, dh).transpose(1, 0, 2)
    half = max(1, heads // 2)
    side = slot // half
    halves_of = [g[i : i + half] for g in groups for i in range(0, heads, half)]
    across = [(g[i], g[(i + half) % heads]) for g in groups for i in range(heads)]
    theirs = lax.dynamic_slice_in_dim(packed, (1 - side) * half, half, 0)
    theirs = lax.ppermute(theirs, both, across)
    mine = lax.dynamic_slice_in_dim(packed, side * half, half, 0)
    asked = call(merge_kernel, struct((half, 2, tokens, dh), BF16), (mine, theirs))
    weights = lax.dynamic_index_in_dim(fast_weights, slot, 1, keepdims=False)
    chunk = max(c for c in (1, 2, 4) if heads % c == 0)
    split = 2 if ff % (2 * LANES) == 0 else 1
    width = ff // split
    coded = count == 2
    partials = []
    for start in range(0, ff, width):
        sums = struct((kinds, dh, width), F32)
        rows = kinds * dh * width // LANES + code_rows(kinds * width // LANES)
        partial = call(
            functools.partial(gradient_kernel, max(1, chunk // 2), start),
            struct((rows, LANES), jnp.int16) if coded else sums,
            (received, weights),
            flops=2**32,
            limit=16,
            scratch=[pltpu.VMEM(sums.shape, F32)] if coded else [],
        )
        partials.append(partial)

    asked = lax.all_to_all(asked, both, 0, 0, tiled=True, axis_index_groups=halves_of)
    if coded:
        parts = [x for code in partials for x in (code, lax.ppermute(code, both, turn))]
    else:
        same = [[g * heads + i for g in range(count)] for i in range(heads)]
        parts = lax.psum(tuple(partials), "tok", axis_index_groups=same)
    new = call(
        functools.partial(update_kernel, ITERS, coded),
        struct((kinds, dh, ff), BF16),
        (slot.reshape(1), step_size, *parts, weights),
        scalars=2,
        flops=2**33,
    )
    read = call(
        functools.partial(read_kernel, max(1, chunk // 2)),
        struct((heads, tokens, dh), BF16),
        (side.reshape(1), new, asked),
        scalars=1,
        limit=16,
    )

    places = sorted(range(heads), key=lambda i: spot(i // half, i % half, half))
    reads = lax.all_to_all(
        read, both, 0, 0, tiled=True, axis_index_groups=[[g[i] for i in places] for g in groups]
    )
    pieces = [
        lax.ppermute(reads, "head", [(i, (i + s) % head_size) for i in range(head_size)])
        for s in range(1, head_size)
    ]
    columns = out_proj.shape[1]
    depth = heads * dh
    own, *rest = call(
        project_own_kernel,
        (
            struct((tokens, columns), F32),
            *[struct((depth, columns), BF16) for _ in range(1, head_size)],
        ),
        (column.reshape(1), reads, out_proj),
        scalars=1,
        hbm=(2,),
        limit=49,
        scratch=[pltpu.VMEM((depth, columns), BF16), pltpu.SemaphoreType.DMA((head_size,))],
    )
    shares = max(c for c in (1, 2, 4) if columns % (c * LANES) == 0)
    return call(
        project_rest_kernel,
        struct((tokens, columns), BF16),
        (own, *pieces, *rest),
        hbm=(-1,),
        scratch=[pltpu.VMEM((tokens, columns), BF16), pltpu.SemaphoreType.DMA((shares,))],
    )


def solution(mesh):
    sizes = dict(mesh.shape)
    in_specs = (
        P("tok", "head"),
        P("tok", "head"),
        P("tok", "head"),
        P(None, "head", None, None),
        P("head"),
        P("tok"),
        P(None, "head"),
    )
    return jax.shard_map(
        functools.partial(on_device, sizes["tok"], sizes["head"]),
        mesh=mesh,
        in_specs=in_specs,
        out_specs=P("tok", "head"),
        check_vma=False,
    )
```

```python
import functools

import jax
import jax.numpy as jnp
from jax import lax
from jax.experimental import pallas as pl
from jax.experimental.pallas import tpu as pltpu
from jax.sharding import PartitionSpec as P

ITERS = 5
COEF_A = 3.4445
COEF_B = -4.775
COEF_C = 2.0315
BF16 = jnp.bfloat16
F32 = jnp.float32
LANES = 128
KINDS = 3
NN = (((1,), (0,)), ((), ()))
NT = (((1,), (1,)), ((), ()))
TN = (((0,), (0,)), ((), ()))


def dot(a, b, dims=NN):
    return lax.dot_general(a, b, dims, preferred_element_type=F32)


def halves(x):
    high = x.astype(BF16)
    return high, (x - high.astype(F32)).astype(BF16)


def sigmoid(x):
    return 0.5 + 0.5 * jnp.tanh(0.5 * x)


def pack_kernel(mask_ref, keys_ref, values_ref, pairs_ref, wide_ref, kept_ref, mask_kept, in_sem, out_sem, mask_sem):
    heads, _, tokens, dh = pairs_ref.shape
    blocks = mask_ref.shape[1]
    shares = in_sem.shape[1]
    length = tokens // shares
    sources = (keys_ref, values_ref)
    mask_copy = pltpu.make_async_copy(mask_ref, mask_kept, mask_sem)
    mask_copy.start()
    loads, stores = [], []
    for r in range(shares):
        rows = pl.ds(r * length, length)
        for p in range(2):
            loads.append(
                pltpu.make_async_copy(sources[p].at[rows], wide_ref.at[p, rows], in_sem.at[p, r])
            )
            loads[-1].start()
    mask_copy.wait()
    for r in range(shares):
        rows = pl.ds(r * length, length)
        for p in range(2):
            loads[2 * r + p].wait()
            for i in range(heads):
                columns = pl.ds(i * dh, dh)
                if p == 0:
                    kept_ref[i, p, rows] = wide_ref[p, rows, columns]
                    continue
                size = min(length, tokens // blocks)
                for start in range(r * length, (r + 1) * length, size):
                    some = pl.ds(start, size)
                    b = start // (tokens // blocks)
                    kept = wide_ref[p, some, columns].astype(F32) * mask_kept[:, b : b + 1].astype(F32)
                    kept_ref[i, p, some] = kept.astype(BF16)
            stores.append(
                pltpu.make_async_copy(
                    kept_ref.at[:, p, rows], pairs_ref.at[:, p, rows], out_sem.at[p, r]
                )
            )
            stores[-1].start()
    for store in stores:
        store.wait()


def gradient_kernel(chunk, start, recv_ref, weights_ref, out_ref, *scratch):
    sources, _, sub, dh = recv_ref.shape
    grads_ref = scratch[0] if scratch else out_ref
    ff = grads_ref.shape[-1]
    units = pl.ds(start, ff)
    gate_up = jnp.concatenate([weights_ref[0, :, units], weights_ref[2, :, units]], axis=1).astype(BF16)
    down = weights_ref[1, :, units].astype(BF16)
    for i in range(0, sources, chunk):
        rows = pl.ds(i, chunk)
        keys = recv_ref[rows, 0].reshape(chunk * sub, dh)
        values = recv_ref[rows, 1].reshape(chunk * sub, dh)
        pre = dot(keys, gate_up)
        gate, up = pre[:, :ff], pre[:, ff:]
        back = dot(values, down)
        sig = sigmoid(gate)
        act = gate * sig
        hidden = (act * up).astype(BF16)
        gate_grad = (back * up * (sig + act * (1.0 - sig))).astype(BF16)
        up_grad = (back * act).astype(BF16)
        sums = dot(keys.T, jnp.concatenate([gate_grad, up_grad], axis=1))
        sums = (sums[:, :ff], dot(values.T, hidden), sums[:, ff:])
        for m, value in enumerate(sums):
            grads_ref[m] = value if i == 0 else grads_ref[m] + value
    if scratch:
        encode(grads_ref, out_ref)


def encode(grads_ref, coded_ref):
    kinds, dh, ff = grads_ref.shape
    powers = []
    for m in range(kinds):
        for c in range(ff // LANES):
            block = grads_ref[m, :, c * LANES : (c + 1) * LANES]
            top = jnp.max(jnp.abs(block), axis=0, keepdims=True)
            power = jnp.floor(jnp.log2(jnp.maximum(top, 1e-30))) - 14.0
            code = jnp.clip(jnp.round(block * jnp.exp2(-power)), -32767.0, 32767.0)
            coded_ref[pl.ds(len(powers) * dh, dh)] = code.astype(jnp.int32).astype(jnp.int16)
            powers.append(power)
    rest = coded_ref.shape[0] - len(powers) * dh
    powers += [jnp.zeros_like(powers[0])] * (rest - len(powers))
    power = jnp.concatenate(powers, axis=0)
    coded_ref[pl.ds(coded_ref.shape[0] - rest, rest)] = power.astype(jnp.int32).astype(jnp.int16)


def decode(coded_ref, m, dh, ff):
    width = ff // LANES
    rest = code_rows(KINDS * width)
    power = coded_ref[pl.ds(coded_ref.shape[0] - rest, rest)].astype(jnp.int32).astype(F32)
    blocks = []
    for c in range(width):
        i = m * width + c
        code = coded_ref[pl.ds(i * dh, dh)].astype(jnp.int32).astype(F32)
        blocks.append(code * jnp.exp2(power[i : i + 1]))
    return jnp.concatenate(blocks, axis=1)


def code_rows(columns):
    return -(-columns // 16) * 16


def square_product(a, b):
    (ah, al), (bh, bl) = a, b
    size = bh.shape[1]
    wide = jnp.concatenate([bh, bl], axis=1)
    both = dot(jnp.concatenate([ah, al], axis=1), jnp.concatenate([wide, wide], axis=0))
    return both[:, :size] + both[:, size:]


def product(a, b):
    (ah, al), (bh, bl) = a, b
    return dot(jnp.concatenate([ah, al], axis=1), jnp.concatenate([bh, bh], axis=0)) + dot(ah, bl)


def gram(x):
    high, low = x
    size = high.shape[0]
    both = dot(high, jnp.concatenate([high, low], axis=0), NT)
    cross = both[:, size:]
    return both[:, :size] + (cross + cross.T)


def newton_schulz(grads, iters):
    size = grads[0].shape[0]
    lines = lax.broadcasted_iota(jnp.int32, (size, size), 0)
    diagonal = lines == lax.broadcasted_iota(jnp.int32, (size, size), 1)
    split = [halves(x) for x in grads]
    grams = [gram(x) for x in split]
    scales = [
        1.0 / (jnp.sum(jnp.where(diagonal, a, 0.0), axis=(0, 1), keepdims=True) + 1e-06)
        for a in grams
    ]
    grams = [a * scale for a, scale in zip(grams, scales)]
    parts = [halves(a) for a in grams]
    polys = [halves(COEF_B * a + COEF_C * square_product(p, p)) for a, p in zip(grams, parts)]
    iterates = [
        (COEF_A * x + product(p, s)) * jnp.sqrt(scale)
        for x, p, s, scale in zip(grads, polys, split, scales)
    ]
    split = [halves(x) for x in iterates]
    grams = [gram(x) for x in split]
    steps = None
    for left in range(iters - 2, -1, -1):
        parts = [halves(a) for a in grams]
        polys = [
            halves(jnp.where(diagonal, COEF_A, 0.0) + (COEF_B * a + COEF_C * square_product(p, p)))
            for a, p in zip(grams, parts)
        ]
        if left > 0:
            inner = [halves(square_product(p, a)) for p, a in zip(polys, parts)]
            grams = [square_product(a, p) for a, p in zip(inner, polys)]
            if steps is None:
                steps = polys
            else:
                steps = [halves(square_product(p, q)) for p, q in zip(polys, steps)]
        if left == 1:
            split = [halves(product(q, s)) for q, s in zip(steps, split)]
    return [product(p, s) for p, s in zip(polys, split)]


def update_kernel(iters, coded, slot_ref, rate_ref, *refs):
    parts, (weights_ref, new_ref) = refs[:-2], refs[-2:]
    kinds, dh, ff = weights_ref.shape
    rate = rate_ref[slot_ref[0]]
    iterates = []
    for m in range(kinds):
        if coded:
            width = ff // (len(parts) // 2)
            blocks = [
                decode(own, m, dh, width) + decode(other, m, dh, width)
                for own, other in zip(parts[::2], parts[1::2])
            ]
        else:
            blocks = [part[m] for part in parts]
        iterates.append(jnp.concatenate(blocks, axis=1))
    iterates = newton_schulz(iterates, iters)
    for m in range(kinds):
        old = weights_ref[m]
        new = old + rate * iterates[m]
        old_norm = jnp.sqrt(jnp.sum(old * old, axis=0, keepdims=True) + 1e-06)
        new_norm = jnp.sqrt(jnp.sum(new * new, axis=0, keepdims=True) + 1e-06)
        new_ref[m] = (new * (old_norm / new_norm)).astype(BF16)


def merge_kernel(mine_ref, theirs_ref, both_ref):
    both_ref[:, 0] = mine_ref[...]
    both_ref[:, 1] = theirs_ref[...]


def read_kernel(chunk, side_ref, new_ref, query_ref, read_ref):
    half, sides, sub, dh = query_ref.shape
    ff = new_ref.shape[-1]
    gate_up = jnp.concatenate([new_ref[0], new_ref[2]], axis=1)
    down = new_ref[1]

    for i in range(0, half, chunk):
        pre = dot(query_ref[pl.ds(i, chunk)].reshape(chunk * sides * sub, dh), gate_up)
        gate, up = pre[:, :ff], pre[:, ff:]
        hidden = (gate * sigmoid(gate) * up).astype(BF16)
        read = dot(hidden, down, NT).astype(BF16).reshape(chunk, sides, sub, dh)
        for c in range(chunk):
            read_ref[spot(side_ref[0], i + c, half)] = read[c, 0]
            if sides == 2:
                read_ref[spot(1 - side_ref[0], i + c, half)] = read[c, 1]


def spot(side, i, half):
    if half % 2 == 0:
        return (half // 2 - 1 - i // 2) * 4 + side * 2 + 1 - i % 2
    return side * half + half - 1 - i


def flat_heads(read_ref):
    heads = read_ref.shape[0]
    half = max(1, heads // 2)
    return jnp.concatenate([read_ref[spot(i // half, i % half, half)] for i in range(heads)], axis=1)


def project_own_kernel(column_ref, read_ref, weight_ref, sum_ref, *refs):
    rest_refs, (own_ref, sems) = refs[:-2], refs[-2:]
    depth, columns = own_ref.shape
    size = weight_ref.shape[0] // depth
    shares = sems.shape[1]
    length = depth // shares
    copies = []
    for s, target in enumerate((own_ref, *rest_refs)):
        base = lax.rem(column_ref[0] + size - s, size) * depth
        for i in range(shares):
            rows = pl.ds(pl.multiple_of(base + i * length, length), length)
            part = target.at[pl.ds(i * length, length)]
            copies.append(pltpu.make_async_copy(weight_ref.at[rows], part, sems.at[s, i]))
            copies[-1].start()
    flat = flat_heads(read_ref)
    for i in range(shares):
        copies[i].wait()
        rows = slice(i * length, (i + 1) * length)
        value = dot(flat[:, rows], own_ref[rows])
        sum_ref[...] = value if i == 0 else sum_ref[...] + value
    for copy in copies[shares:]:
        copy.wait()


def project_rest_kernel(sum_ref, *refs):
    refs, (out_ref, held_ref, sems) = refs[:-3], refs[-3:]
    reads, weights = refs[: len(refs) // 2], refs[len(refs) // 2 :]
    flats = [flat_heads(read) for read in reads]
    shares = sems.shape[0]
    width = held_ref.shape[1] // shares
    copies = []
    for i in range(shares):
        columns = pl.ds(i * width, width)
        value = sum_ref[:, columns]
        for flat, weight in zip(flats, weights):
            value = value + dot(flat, weight[:, columns])
        held_ref[:, columns] = (value * sigmoid(value)).astype(BF16)
        copies.append(
            pltpu.make_async_copy(held_ref.at[:, columns], out_ref.at[:, columns], sems.at[i])
        )
        copies[-1].start()
    for copy in copies:
        copy.wait()


def call(kernel, out_shape, args, scalars=0, flops=None, limit=12, hbm=(), scratch=()):
    specs = [pl.BlockSpec(memory_space=pltpu.SMEM)] * scalars
    specs += [
        pl.BlockSpec(memory_space=pl.ANY if i in hbm else pltpu.VMEM)
        for i in range(scalars, len(args))
    ]
    cost = None
    if flops is not None:
        cost = pl.CostEstimate(flops=flops, bytes_accessed=2**20, transcendentals=0)
    return pl.pallas_call(
        kernel,
        out_shape=out_shape,
        in_specs=specs,
        out_specs=jax.tree.map(
            lambda _: pl.BlockSpec(memory_space=pl.ANY if -1 in hbm else pltpu.VMEM), out_shape
        ),
        scratch_shapes=list(scratch),
        compiler_params=pltpu.CompilerParams(vmem_limit_bytes=limit * 2**20),
        cost_estimate=cost,
    )(*args)


def on_device(tok_size, head_size, keys, values, queries, fast_weights, step_size, edit_mask, out_proj):
    tokens = keys.shape[0]
    kinds, heads, dh, ff = fast_weights.shape
    column = lax.axis_index("head")
    place = lax.axis_index("tok")
    count = tok_size // heads
    struct = jax.ShapeDtypeStruct
    both = ("tok", "head")

    quarter = tok_size // 4
    mixed = count == 2 and quarter * 4 == tok_size and head_size % 2 == 0
    slot = place % heads
    groups, turn = [], []
    for h in range(head_size):
        if mixed and h % 2 == 1:
            order = [q * quarter + i for q in (0, 2, 1, 3) for i in range(quarter)]
            partners = [t + quarter if t // quarter % 2 == 0 else t - quarter for t in range(tok_size)]
        else:
            order = list(range(tok_size))
            partners = [(t + heads) % tok_size for t in range(tok_size)]
        for g in range(count):
            groups.append([t * head_size + h for t in order[g * heads : (g + 1) * heads]])
        turn += [(t * head_size + h, partners[t] * head_size + h) for t in range(tok_size)]
    if mixed:
        other = place % quarter + quarter * (place // (2 * quarter))
        slot = jnp.where(column % 2 == 1, other, slot)
    turned = heads // 2
    groups = [g[turned:] + g[:turned] for g in groups]
    slot = (slot + heads - turned) % heads

    pairs = call(
        pack_kernel,
        struct((heads, 2, tokens, dh), BF16),
        (edit_mask[None], keys, values),
        hbm=(-1, 0, 1, 2),
        limit=60,
        scratch=[
            pltpu.VMEM((2, tokens, heads * dh), BF16),
            pltpu.VMEM((heads, 2, tokens, dh), BF16),
            pltpu.VMEM((1, *edit_mask.shape), edit_mask.dtype),
            pltpu.SemaphoreType.DMA((2, 2)),
            pltpu.SemaphoreType.DMA((2, 2)),
            pltpu.SemaphoreType.DMA,
        ],
    )
    received = lax.all_to_all(pairs, both, 0, 0, tiled=True, axis_index_groups=groups)
    packed = queries.reshape(tokens, heads, dh).transpose(1, 0, 2)
    half = max(1, heads // 2)
    side = slot // half
    halves_of = [g[i : i + half] for g in groups for i in range(0, heads, half)]
    across = [(g[i], g[(i + half) % heads]) for g in groups for i in range(heads)]
    theirs = lax.dynamic_slice_in_dim(packed, (1 - side) * half, half, 0)
    theirs = lax.ppermute(theirs, both, across)
    mine = lax.dynamic_slice_in_dim(packed, side * half, half, 0)
    asked = call(merge_kernel, struct((half, 2, tokens, dh), BF16), (mine, theirs))
    weights = lax.dynamic_index_in_dim(fast_weights, slot, 1, keepdims=False)
    chunk = max(c for c in (1, 2, 4) if heads % c == 0)
    split = 2 if ff % (2 * LANES) == 0 else 1
    width = ff // split
    coded = count == 2
    partials = []
    for start in range(0, ff, width):
        sums = struct((kinds, dh, width), F32)
        rows = kinds * dh * width // LANES + code_rows(kinds * width // LANES)
        partial = call(
            functools.partial(gradient_kernel, max(1, chunk // 2), start),
            struct((rows, LANES), jnp.int16) if coded else sums,
            (received, weights),
            flops=2**32,
            limit=16,
            scratch=[pltpu.VMEM(sums.shape, F32)] if coded else [],
        )
        partials.append(partial)

    asked = lax.all_to_all(asked, both, 0, 0, tiled=True, axis_index_groups=halves_of)
    if coded:
        parts = [x for code in partials for x in (code, lax.ppermute(code, both, turn))]
    else:
        same = [[g * heads + i for g in range(count)] for i in range(heads)]
        parts = lax.psum(tuple(partials), "tok", axis_index_groups=same)
    new = call(
        functools.partial(update_kernel, ITERS, coded),
        struct((kinds, dh, ff), BF16),
        (slot.reshape(1), step_size, *parts, weights),
        scalars=2,
        flops=2**33,
    )
    read = call(
        functools.partial(read_kernel, 1),
        struct((heads, tokens, dh), BF16),
        (side.reshape(1), new, asked),
        scalars=1,
        limit=16,
    )

    places = sorted(range(heads), key=lambda i: spot(i // half, i % half, half))
    reads = lax.all_to_all(
        read, both, 0, 0, tiled=True, axis_index_groups=[[g[i] for i in places] for g in groups]
    )
    pieces = [
        lax.ppermute(reads, "head", [(i, (i + s) % head_size) for i in range(head_size)])
        for s in range(1, head_size)
    ]
    columns = out_proj.shape[1]
    depth = heads * dh
    parts_of = max(c for c in (1, 2, 4) if depth % (c * LANES) == 0)
    own, *rest = call(
        project_own_kernel,
        (
            struct((tokens, columns), F32),
            *[struct((depth, columns), BF16) for _ in range(1, head_size)],
        ),
        (column.reshape(1), reads, out_proj),
        scalars=1,
        hbm=(2,),
        limit=49,
        scratch=[pltpu.VMEM((depth, columns), BF16), pltpu.SemaphoreType.DMA((head_size, parts_of))],
    )
    shares = max(c for c in (1, 2, 4) if columns % (c * LANES) == 0)
    return call(
        project_rest_kernel,
        struct((tokens, columns), BF16),
        (own, *pieces, *rest),
        hbm=(-1,),
        scratch=[pltpu.VMEM((tokens, columns), BF16), pltpu.SemaphoreType.DMA((shares,))],
    )


def solution(mesh):
    sizes = dict(mesh.shape)
    in_specs = (
        P("tok", "head"),
        P("tok", "head"),
        P("tok", "head"),
        P(None, "head", None, None),
        P("head"),
        P("tok"),
        P(None, "head"),
    )
    return jax.shard_map(
        functools.partial(on_device, sizes["tok"], sizes["head"]),
        mesh=mesh,
        in_specs=in_specs,
        out_specs=P("tok", "head"),
        check_vma=False,
    )
```

```python
import functools

import jax
import jax.numpy as jnp
from jax import lax
from jax.experimental import pallas as pl
from jax.experimental.pallas import tpu as pltpu
from jax.sharding import PartitionSpec as P

ITERS = 5
COEF_A = 3.4445
COEF_B = -4.775
COEF_C = 2.0315
BF16 = jnp.bfloat16
F32 = jnp.float32
LANES = 128
KINDS = 3
NN = (((1,), (0,)), ((), ()))
NT = (((1,), (1,)), ((), ()))
TN = (((0,), (0,)), ((), ()))


def dot(a, b, dims=NN):
    return lax.dot_general(a, b, dims, preferred_element_type=F32)


def halves(x):
    high = x.astype(BF16)
    return high, (x - high.astype(F32)).astype(BF16)


def sigmoid(x):
    return 0.5 + 0.5 * jnp.tanh(0.5 * x)


def pack_kernel(mask_ref, keys_ref, values_ref, pairs_ref, wide_ref, kept_ref, mask_kept, in_sem, out_sem, mask_sem):
    heads, _, tokens, dh = pairs_ref.shape
    blocks = mask_ref.shape[1]
    shares = in_sem.shape[1]
    length = tokens // shares
    sources = (keys_ref, values_ref)
    mask_copy = pltpu.make_async_copy(mask_ref, mask_kept, mask_sem)
    mask_copy.start()
    loads, stores = [], []
    for r in range(shares):
        rows = pl.ds(r * length, length)
        for p in range(2):
            loads.append(
                pltpu.make_async_copy(sources[p].at[rows], wide_ref.at[p, rows], in_sem.at[p, r])
            )
            loads[-1].start()
    mask_copy.wait()
    for r in range(shares):
        rows = pl.ds(r * length, length)
        for p in range(2):
            loads[2 * r + p].wait()
            for i in range(heads):
                columns = pl.ds(i * dh, dh)
                if p == 0:
                    kept_ref[i, p, rows] = wide_ref[p, rows, columns]
                    continue
                size = min(length, tokens // blocks)
                for start in range(r * length, (r + 1) * length, size):
                    some = pl.ds(start, size)
                    b = start // (tokens // blocks)
                    kept = wide_ref[p, some, columns].astype(F32) * mask_kept[:, b : b + 1].astype(F32)
                    kept_ref[i, p, some] = kept.astype(BF16)
            stores.append(
                pltpu.make_async_copy(
                    kept_ref.at[:, p, rows], pairs_ref.at[:, p, rows], out_sem.at[p, r]
                )
            )
            stores[-1].start()
    for store in stores:
        store.wait()


def gradient_kernel(chunk, start, recv_ref, weights_ref, out_ref, *scratch):
    sources, _, sub, dh = recv_ref.shape
    grads_ref = scratch[0] if scratch else out_ref
    ff = grads_ref.shape[-1]
    units = pl.ds(start, ff)
    gate_up = jnp.concatenate([weights_ref[0, :, units], weights_ref[2, :, units]], axis=1)
    down = weights_ref[1, :, units]
    for i in range(0, sources, chunk):
        rows = pl.ds(i, chunk)
        keys = recv_ref[rows, 0].reshape(chunk * sub, dh)
        values = recv_ref[rows, 1].reshape(chunk * sub, dh)
        pre = dot(keys, gate_up)
        gate, up = pre[:, :ff], pre[:, ff:]
        back = dot(values, down)
        sig = sigmoid(gate)
        act = gate * sig
        hidden = (act * up).astype(BF16)
        gate_grad = (back * up * (sig + act * (1.0 - sig))).astype(BF16)
        up_grad = (back * act).astype(BF16)
        sums = dot(keys.T, jnp.concatenate([gate_grad, up_grad], axis=1))
        sums = (sums[:, :ff], dot(values.T, hidden), sums[:, ff:])
        for m, value in enumerate(sums):
            grads_ref[m] = value if i == 0 else grads_ref[m] + value
    if scratch:
        encode(grads_ref, out_ref)


def encode(grads_ref, coded_ref):
    kinds, dh, ff = grads_ref.shape
    powers = []
    for m in range(kinds):
        for c in range(ff // LANES):
            block = grads_ref[m, :, c * LANES : (c + 1) * LANES]
            top = jnp.max(jnp.abs(block), axis=0, keepdims=True)
            power = jnp.floor(jnp.log2(jnp.maximum(top, 1e-30))) - 14.0
            code = jnp.clip(jnp.round(block * jnp.exp2(-power)), -32767.0, 32767.0)
            coded_ref[pl.ds(len(powers) * dh, dh)] = code.astype(jnp.int32).astype(jnp.int16)
            powers.append(power)
    rest = coded_ref.shape[0] - len(powers) * dh
    powers += [jnp.zeros_like(powers[0])] * (rest - len(powers))
    power = jnp.concatenate(powers, axis=0)
    coded_ref[pl.ds(coded_ref.shape[0] - rest, rest)] = power.astype(jnp.int32).astype(jnp.int16)


def decode(coded_ref, m, dh, ff):
    width = ff // LANES
    rest = code_rows(KINDS * width)
    power = coded_ref[pl.ds(coded_ref.shape[0] - rest, rest)].astype(jnp.int32).astype(F32)
    blocks = []
    for c in range(width):
        i = m * width + c
        code = coded_ref[pl.ds(i * dh, dh)].astype(jnp.int32).astype(F32)
        blocks.append(code * jnp.exp2(power[i : i + 1]))
    return jnp.concatenate(blocks, axis=1)


def code_rows(columns):
    return -(-columns // 16) * 16


def square_product(a, b):
    (ah, al), (bh, bl) = a, b
    size = bh.shape[1]
    wide = jnp.concatenate([bh, bl], axis=1)
    both = dot(jnp.concatenate([ah, al], axis=1), jnp.concatenate([wide, wide], axis=0))
    return both[:, :size] + both[:, size:]


def product(a, b):
    (ah, al), (bh, bl) = a, b
    return dot(jnp.concatenate([ah, al], axis=1), jnp.concatenate([bh, bh], axis=0)) + dot(ah, bl)


def gram(x):
    high, low = x
    size = high.shape[0]
    both = dot(high, jnp.concatenate([high, low], axis=0), NT)
    cross = both[:, size:]
    return both[:, :size] + (cross + cross.T)


def newton_schulz(grads, iters):
    size = grads[0].shape[0]
    lines = lax.broadcasted_iota(jnp.int32, (size, size), 0)
    diagonal = lines == lax.broadcasted_iota(jnp.int32, (size, size), 1)
    split = [halves(x) for x in grads]
    grams = [gram(x) for x in split]
    scales = [
        1.0 / (jnp.sum(jnp.where(diagonal, a, 0.0), axis=(0, 1), keepdims=True) + 1e-06)
        for a in grams
    ]
    grams = [a * scale for a, scale in zip(grams, scales)]
    parts = [halves(a) for a in grams]
    polys = [halves(COEF_B * a + COEF_C * square_product(p, p)) for a, p in zip(grams, parts)]
    iterates = [
        (COEF_A * x + product(p, s)) * jnp.sqrt(scale)
        for x, p, s, scale in zip(grads, polys, split, scales)
    ]
    split = [halves(x) for x in iterates]
    grams = [gram(x) for x in split]
    steps = None
    for left in range(iters - 2, -1, -1):
        parts = [halves(a) for a in grams]
        polys = [
            halves(jnp.where(diagonal, COEF_A, 0.0) + (COEF_B * a + COEF_C * square_product(p, p)))
            for a, p in zip(grams, parts)
        ]
        if left > 0:
            inner = [halves(square_product(p, a)) for p, a in zip(polys, parts)]
            grams = [square_product(a, p) for a, p in zip(inner, polys)]
            if steps is None:
                steps = polys
            else:
                steps = [halves(square_product(p, q)) for p, q in zip(polys, steps)]
        if left == 1:
            split = [halves(product(q, s)) for q, s in zip(steps, split)]
    return [product(p, s) for p, s in zip(polys, split)]


def update_kernel(iters, coded, slot_ref, rate_ref, *refs):
    parts, (weights_ref, new_ref) = refs[:-2], refs[-2:]
    kinds, dh, ff = weights_ref.shape
    rate = rate_ref[slot_ref[0]]
    iterates = []
    for m in range(kinds):
        if coded:
            width = ff // (len(parts) // 2)
            blocks = [
                decode(own, m, dh, width) + decode(other, m, dh, width)
                for own, other in zip(parts[::2], parts[1::2])
            ]
        else:
            blocks = [part[m] for part in parts]
        iterates.append(jnp.concatenate(blocks, axis=1))
    iterates = newton_schulz(iterates, iters)
    for m in range(kinds):
        old = weights_ref[m]
        new = old + rate * iterates[m]
        old_norm = jnp.sqrt(jnp.sum(old * old, axis=0, keepdims=True) + 1e-06)
        new_norm = jnp.sqrt(jnp.sum(new * new, axis=0, keepdims=True) + 1e-06)
        new_ref[m] = (new * (old_norm / new_norm)).astype(BF16)


def merge_kernel(mine_ref, theirs_ref, both_ref):
    both_ref[:, 0] = mine_ref[...]
    both_ref[:, 1] = theirs_ref[...]


def read_kernel(chunk, side_ref, new_ref, query_ref, read_ref):
    half, sides, sub, dh = query_ref.shape
    ff = new_ref.shape[-1]
    gate_up = jnp.concatenate([new_ref[0], new_ref[2]], axis=1)
    down = new_ref[1]

    for i in range(0, half, chunk):
        pre = dot(query_ref[pl.ds(i, chunk)].reshape(chunk * sides * sub, dh), gate_up)
        gate, up = pre[:, :ff], pre[:, ff:]
        hidden = (gate * sigmoid(gate) * up).astype(BF16)
        read = dot(hidden, down, NT).astype(BF16).reshape(chunk, sides, sub, dh)
        for c in range(chunk):
            read_ref[spot(side_ref[0], i + c, half)] = read[c, 0]
            if sides == 2:
                read_ref[spot(1 - side_ref[0], i + c, half)] = read[c, 1]


def spot(side, i, half):
    if half % 2 == 0:
        return (half // 2 - 1 - i // 2) * 4 + side * 2 + 1 - i % 2
    return side * half + half - 1 - i


def flat_heads(read_ref):
    heads = read_ref.shape[0]
    half = max(1, heads // 2)
    return jnp.concatenate([read_ref[spot(i // half, i % half, half)] for i in range(heads)], axis=1)


def project_own_kernel(column_ref, read_ref, weight_ref, sum_ref, *refs):
    rest_refs, (own_ref, sems) = refs[:-2], refs[-2:]
    depth, columns = own_ref.shape
    size = weight_ref.shape[0] // depth
    shares = sems.shape[1]
    length = depth // shares
    copies = []
    for s, target in enumerate((own_ref, *rest_refs)):
        base = lax.rem(column_ref[0] + size - s, size) * depth
        for i in range(shares):
            rows = pl.ds(pl.multiple_of(base + i * length, length), length)
            part = target.at[pl.ds(i * length, length)]
            copies.append(pltpu.make_async_copy(weight_ref.at[rows], part, sems.at[s, i]))
            copies[-1].start()
    flat = flat_heads(read_ref)
    for i in range(shares):
        copies[i].wait()
        rows = slice(i * length, (i + 1) * length)
        value = dot(flat[:, rows], own_ref[rows])
        sum_ref[...] = value if i == 0 else sum_ref[...] + value
    for copy in copies[shares:]:
        copy.wait()


def project_rest_kernel(sum_ref, *refs):
    refs, (out_ref, held_ref, sems) = refs[:-3], refs[-3:]
    reads, weights = refs[: len(refs) // 2], refs[len(refs) // 2 :]
    flats = [flat_heads(read) for read in reads]
    shares = sems.shape[0]
    width = held_ref.shape[1] // shares
    copies = []
    for i in range(shares):
        columns = pl.ds(i * width, width)
        value = sum_ref[:, columns]
        for flat, weight in zip(flats, weights):
            value = value + dot(flat, weight[:, columns])
        held_ref[:, columns] = (value * sigmoid(value)).astype(BF16)
        copies.append(
            pltpu.make_async_copy(held_ref.at[:, columns], out_ref.at[:, columns], sems.at[i])
        )
        copies[-1].start()
    for copy in copies:
        copy.wait()


def call(kernel, out_shape, args, scalars=0, flops=None, limit=12, hbm=(), scratch=()):
    specs = [pl.BlockSpec(memory_space=pltpu.SMEM)] * scalars
    specs += [
        pl.BlockSpec(memory_space=pl.ANY if i in hbm else pltpu.VMEM)
        for i in range(scalars, len(args))
    ]
    cost = None
    if flops is not None:
        cost = pl.CostEstimate(flops=flops, bytes_accessed=2**20, transcendentals=0)
    return pl.pallas_call(
        kernel,
        out_shape=out_shape,
        in_specs=specs,
        out_specs=jax.tree.map(
            lambda _: pl.BlockSpec(memory_space=pl.ANY if -1 in hbm else pltpu.VMEM), out_shape
        ),
        scratch_shapes=list(scratch),
        compiler_params=pltpu.CompilerParams(vmem_limit_bytes=limit * 2**20),
        cost_estimate=cost,
    )(*args)


def on_device(tok_size, head_size, keys, values, queries, fast_weights, step_size, edit_mask, out_proj):
    tokens = keys.shape[0]
    kinds, heads, dh, ff = fast_weights.shape
    column = lax.axis_index("head")
    place = lax.axis_index("tok")
    count = tok_size // heads
    struct = jax.ShapeDtypeStruct
    both = ("tok", "head")

    quarter = tok_size // 4
    mixed = count == 2 and quarter * 4 == tok_size and head_size % 2 == 0
    slot = place % heads
    groups, turn = [], []
    for h in range(head_size):
        if mixed and h % 2 == 1:
            order = [q * quarter + i for q in (0, 2, 1, 3) for i in range(quarter)]
            partners = [t + quarter if t // quarter % 2 == 0 else t - quarter for t in range(tok_size)]
        else:
            order = list(range(tok_size))
            partners = [(t + heads) % tok_size for t in range(tok_size)]
        for g in range(count):
            groups.append([t * head_size + h for t in order[g * heads : (g + 1) * heads]])
        turn += [(t * head_size + h, partners[t] * head_size + h) for t in range(tok_size)]
    if mixed:
        other = place % quarter + quarter * (place // (2 * quarter))
        slot = jnp.where(column % 2 == 1, other, slot)
    turned = heads // 2
    groups = [g[turned:] + g[:turned] for g in groups]
    slot = (slot + heads - turned) % heads

    pairs = call(
        pack_kernel,
        struct((heads, 2, tokens, dh), BF16),
        (edit_mask[None], keys, values),
        hbm=(-1, 0, 1, 2),
        limit=60,
        scratch=[
            pltpu.VMEM((2, tokens, heads * dh), BF16),
            pltpu.VMEM((heads, 2, tokens, dh), BF16),
            pltpu.VMEM((1, *edit_mask.shape), edit_mask.dtype),
            pltpu.SemaphoreType.DMA((2, 2)),
            pltpu.SemaphoreType.DMA((2, 2)),
            pltpu.SemaphoreType.DMA,
        ],
    )
    received = lax.all_to_all(pairs, both, 0, 0, tiled=True, axis_index_groups=groups)
    packed = queries.reshape(tokens, heads, dh).transpose(1, 0, 2)
    half = max(1, heads // 2)
    side = slot // half
    halves_of = [g[i : i + half] for g in groups for i in range(0, heads, half)]
    across = [(g[i], g[(i + half) % heads]) for g in groups for i in range(heads)]
    theirs = lax.dynamic_slice_in_dim(packed, (1 - side) * half, half, 0)
    theirs = lax.ppermute(theirs, both, across)
    mine = lax.dynamic_slice_in_dim(packed, side * half, half, 0)
    asked = call(merge_kernel, struct((half, 2, tokens, dh), BF16), (mine, theirs))
    weights = lax.dynamic_index_in_dim(fast_weights, slot, 1, keepdims=False)
    chunk = max(c for c in (1, 2, 4) if heads % c == 0)
    split = 2 if ff % (2 * LANES) == 0 else 1
    width = ff // split
    low = weights.astype(BF16)
    coded = count == 2
    partials = []
    for start in range(0, ff, width):
        sums = struct((kinds, dh, width), F32)
        rows = kinds * dh * width // LANES + code_rows(kinds * width // LANES)
        partial = call(
            functools.partial(gradient_kernel, max(1, chunk // 2), start),
            struct((rows, LANES), jnp.int16) if coded else sums,
            (received, low),
            flops=2**32,
            limit=16,
            scratch=[pltpu.VMEM(sums.shape, F32)] if coded else [],
        )
        partials.append(partial)

    asked = lax.all_to_all(asked, both, 0, 0, tiled=True, axis_index_groups=halves_of)
    if coded:
        parts = [x for code in partials for x in (code, lax.ppermute(code, both, turn))]
    else:
        same = [[g * heads + i for g in range(count)] for i in range(heads)]
        parts = lax.psum(tuple(partials), "tok", axis_index_groups=same)
    new = call(
        functools.partial(update_kernel, ITERS, coded),
        struct((kinds, dh, ff), BF16),
        (slot.reshape(1), step_size, *parts, weights),
        scalars=2,
        flops=2**33,
    )
    read = call(
        functools.partial(read_kernel, 1),
        struct((heads, tokens, dh), BF16),
        (side.reshape(1), new, asked),
        scalars=1,
        limit=16,
    )

    places = sorted(range(heads), key=lambda i: spot(i // half, i % half, half))
    reads = lax.all_to_all(
        read, both, 0, 0, tiled=True, axis_index_groups=[[g[i] for i in places] for g in groups]
    )
    pieces = [
        lax.ppermute(reads, "head", [(i, (i + s) % head_size) for i in range(head_size)])
        for s in range(1, head_size)
    ]
    columns = out_proj.shape[1]
    depth = heads * dh
    parts_of = max(c for c in (1, 2, 4) if depth % (c * LANES) == 0)
    own, *rest = call(
        project_own_kernel,
        (
            struct((tokens, columns), F32),
            *[struct((depth, columns), BF16) for _ in range(1, head_size)],
        ),
        (column.reshape(1), reads, out_proj),
        scalars=1,
        hbm=(2,),
        limit=49,
        scratch=[pltpu.VMEM((depth, columns), BF16), pltpu.SemaphoreType.DMA((head_size, parts_of))],
    )
    shares = max(c for c in (1, 2, 4) if columns % (c * LANES) == 0)
    return call(
        project_rest_kernel,
        struct((tokens, columns), BF16),
        (own, *pieces, *rest),
        hbm=(-1,),
        scratch=[pltpu.VMEM((tokens, columns), BF16), pltpu.SemaphoreType.DMA((shares,))],
    )


def solution(mesh):
    sizes = dict(mesh.shape)
    in_specs = (
        P("tok", "head"),
        P("tok", "head"),
        P("tok", "head"),
        P(None, "head", None, None),
        P("head"),
        P("tok"),
        P(None, "head"),
    )
    return jax.shard_map(
        functools.partial(on_device, sizes["tok"], sizes["head"]),
        mesh=mesh,
        in_specs=in_specs,
        out_specs=P("tok", "head"),
        check_vma=False,
    )
```

```python
import functools

import jax
import jax.numpy as jnp
from jax import lax
from jax.experimental import pallas as pl
from jax.experimental.pallas import tpu as pltpu
from jax.sharding import PartitionSpec as P

ITERS = 5
COEF_A = 3.4445
COEF_B = -4.775
COEF_C = 2.0315
BF16 = jnp.bfloat16
F32 = jnp.float32
LANES = 128
KINDS = 3
NN = (((1,), (0,)), ((), ()))
NT = (((1,), (1,)), ((), ()))
TN = (((0,), (0,)), ((), ()))


def dot(a, b, dims=NN):
    return lax.dot_general(a, b, dims, preferred_element_type=F32)


def halves(x):
    high = x.astype(BF16)
    return high, (x - high.astype(F32)).astype(BF16)


def sigmoid(x):
    return 0.5 + 0.5 * jnp.tanh(0.5 * x)


def pack_kernel(mask_ref, keys_ref, values_ref, pairs_ref, wide_ref, kept_ref, mask_kept, in_sem, out_sem, mask_sem):
    heads, _, tokens, dh = pairs_ref.shape
    blocks = mask_ref.shape[1]
    shares = in_sem.shape[1]
    length = tokens // shares
    sources = (keys_ref, values_ref)
    mask_copy = pltpu.make_async_copy(mask_ref, mask_kept, mask_sem)
    mask_copy.start()
    loads, stores = [], []
    for r in range(shares):
        rows = pl.ds(r * length, length)
        for p in range(2):
            loads.append(
                pltpu.make_async_copy(sources[p].at[rows], wide_ref.at[p, rows], in_sem.at[p, r])
            )
            loads[-1].start()
    for r in range(shares):
        rows = pl.ds(r * length, length)
        for p in range(2):
            loads[2 * r + p].wait()
            if r == 0 and p == 1:
                mask_copy.wait()
            for i in range(heads):
                columns = pl.ds(i * dh, dh)
                if p == 0:
                    kept_ref[i, p, rows] = wide_ref[p, rows, columns]
                    continue
                size = min(length, tokens // blocks)
                for start in range(r * length, (r + 1) * length, size):
                    some = pl.ds(start, size)
                    b = start // (tokens // blocks)
                    kept = wide_ref[p, some, columns].astype(F32) * mask_kept[:, b : b + 1].astype(F32)
                    kept_ref[i, p, some] = kept.astype(BF16)
            stores.append(
                pltpu.make_async_copy(
                    kept_ref.at[:, p, rows], pairs_ref.at[:, p, rows], out_sem.at[p, r]
                )
            )
            stores[-1].start()
    for store in stores:
        store.wait()


def gradient_kernel(chunk, start, recv_ref, weights_ref, out_ref, *scratch):
    sources, _, sub, dh = recv_ref.shape
    grads_ref = scratch[0] if scratch else out_ref
    ff = grads_ref.shape[-1]
    units = pl.ds(start, ff)
    gate_up = jnp.concatenate([weights_ref[0, :, units], weights_ref[2, :, units]], axis=1)
    down = weights_ref[1, :, units]
    for i in range(0, sources, chunk):
        rows = pl.ds(i, chunk)
        keys = recv_ref[rows, 0].reshape(chunk * sub, dh)
        values = recv_ref[rows, 1].reshape(chunk * sub, dh)
        pre = dot(keys, gate_up)
        gate, up = pre[:, :ff], pre[:, ff:]
        back = dot(values, down)
        sig = sigmoid(gate)
        act = gate * sig
        hidden = (act * up).astype(BF16)
        gate_grad = (back * up * (sig + act * (1.0 - sig))).astype(BF16)
        up_grad = (back * act).astype(BF16)
        sums = dot(keys.T, jnp.concatenate([gate_grad, up_grad], axis=1))
        sums = (sums[:, :ff], dot(values.T, hidden), sums[:, ff:])
        for m, value in enumerate(sums):
            grads_ref[m] = value if i == 0 else grads_ref[m] + value
    if scratch:
        encode(grads_ref, out_ref)


def encode(grads_ref, coded_ref):
    kinds, dh, ff = grads_ref.shape
    powers = []
    for m in range(kinds):
        for c in range(ff // LANES):
            block = grads_ref[m, :, c * LANES : (c + 1) * LANES]
            top = jnp.max(jnp.abs(block), axis=0, keepdims=True)
            power = jnp.floor(jnp.log2(jnp.maximum(top, 1e-30))) - 14.0
            code = jnp.clip(jnp.round(block * jnp.exp2(-power)), -32767.0, 32767.0)
            coded_ref[pl.ds(len(powers) * dh, dh)] = code.astype(jnp.int32).astype(jnp.int16)
            powers.append(power)
    rest = coded_ref.shape[0] - len(powers) * dh
    powers += [jnp.zeros_like(powers[0])] * (rest - len(powers))
    power = jnp.concatenate(powers, axis=0)
    coded_ref[pl.ds(coded_ref.shape[0] - rest, rest)] = power.astype(jnp.int32).astype(jnp.int16)


def decode(coded_ref, m, dh, ff):
    width = ff // LANES
    rest = code_rows(KINDS * width)
    power = coded_ref[pl.ds(coded_ref.shape[0] - rest, rest)].astype(jnp.int32).astype(F32)
    blocks = []
    for c in range(width):
        i = m * width + c
        code = coded_ref[pl.ds(i * dh, dh)].astype(jnp.int32).astype(F32)
        blocks.append(code * jnp.exp2(power[i : i + 1]))
    return jnp.concatenate(blocks, axis=1)


def code_rows(columns):
    return -(-columns // 16) * 16


def square_product(a, b):
    (ah, al), (bh, bl) = a, b
    size = bh.shape[1]
    wide = jnp.concatenate([bh, bl], axis=1)
    both = dot(jnp.concatenate([ah, al], axis=1), jnp.concatenate([wide, wide], axis=0))
    return both[:, :size] + both[:, size:]


def product(a, b):
    (ah, al), (bh, bl) = a, b
    return dot(jnp.concatenate([ah, al], axis=1), jnp.concatenate([bh, bh], axis=0)) + dot(ah, bl)


def gram(x):
    high, low = x
    size = high.shape[0]
    both = dot(high, jnp.concatenate([high, low], axis=0), NT)
    cross = both[:, size:]
    return both[:, :size] + (cross + cross.T)


def newton_schulz(grads, iters):
    size = grads[0].shape[0]
    lines = lax.broadcasted_iota(jnp.int32, (size, size), 0)
    diagonal = lines == lax.broadcasted_iota(jnp.int32, (size, size), 1)
    split = [halves(x) for x in grads]
    grams = [gram(x) for x in split]
    scales = [
        1.0 / (jnp.sum(jnp.where(diagonal, a, 0.0), axis=(0, 1), keepdims=True) + 1e-06)
        for a in grams
    ]
    grams = [a * scale for a, scale in zip(grams, scales)]
    parts = [halves(a) for a in grams]
    polys = [halves(COEF_B * a + COEF_C * square_product(p, p)) for a, p in zip(grams, parts)]
    iterates = [
        (COEF_A * x + product(p, s)) * jnp.sqrt(scale)
        for x, p, s, scale in zip(grads, polys, split, scales)
    ]
    split = [halves(x) for x in iterates]
    grams = [gram(x) for x in split]
    steps = None
    for left in range(iters - 2, -1, -1):
        parts = [halves(a) for a in grams]
        polys = [
            halves(jnp.where(diagonal, COEF_A, 0.0) + (COEF_B * a + COEF_C * square_product(p, p)))
            for a, p in zip(grams, parts)
        ]
        if left > 0:
            inner = [halves(square_product(p, a)) for p, a in zip(polys, parts)]
            grams = [square_product(a, p) for a, p in zip(inner, polys)]
            if steps is None:
                steps = polys
            else:
                steps = [halves(square_product(p, q)) for p, q in zip(polys, steps)]
        if left == 1:
            split = [halves(product(q, s)) for q, s in zip(steps, split)]
    return [product(p, s) for p, s in zip(polys, split)]


def update_kernel(iters, coded, slot_ref, rate_ref, *refs):
    parts, (weights_ref, new_ref) = refs[:-2], refs[-2:]
    kinds, dh, ff = weights_ref.shape
    rate = rate_ref[slot_ref[0]]
    iterates = []
    for m in range(kinds):
        if coded:
            width = ff // (len(parts) // 2)
            blocks = [
                decode(own, m, dh, width) + decode(other, m, dh, width)
                for own, other in zip(parts[::2], parts[1::2])
            ]
        else:
            blocks = [part[m] for part in parts]
        iterates.append(jnp.concatenate(blocks, axis=1))
    iterates = newton_schulz(iterates, iters)
    for m in range(kinds):
        old = weights_ref[m]
        new = old + rate * iterates[m]
        old_norm = jnp.sqrt(jnp.sum(old * old, axis=0, keepdims=True) + 1e-06)
        new_norm = jnp.sqrt(jnp.sum(new * new, axis=0, keepdims=True) + 1e-06)
        new_ref[m] = (new * (old_norm / new_norm)).astype(BF16)


def merge_kernel(mine_ref, theirs_ref, both_ref):
    both_ref[:, 0] = mine_ref[...]
    both_ref[:, 1] = theirs_ref[...]


def read_kernel(chunk, side_ref, new_ref, query_ref, read_ref):
    half, sides, sub, dh = query_ref.shape
    ff = new_ref.shape[-1]
    gate_up = jnp.concatenate([new_ref[0], new_ref[2]], axis=1)
    down = new_ref[1]

    for i in range(0, half, chunk):
        pre = dot(query_ref[pl.ds(i, chunk)].reshape(chunk * sides * sub, dh), gate_up)
        gate, up = pre[:, :ff], pre[:, ff:]
        hidden = (gate * sigmoid(gate) * up).astype(BF16)
        read = dot(hidden, down, NT).astype(BF16).reshape(chunk, sides, sub, dh)
        for c in range(chunk):
            read_ref[spot(side_ref[0], i + c, half)] = read[c, 0]
            if sides == 2:
                read_ref[spot(1 - side_ref[0], i + c, half)] = read[c, 1]


def spot(side, i, half):
    if half % 2 == 0:
        return (half // 2 - 1 - i // 2) * 4 + side * 2 + 1 - i % 2
    return side * half + half - 1 - i


def flat_heads(read_ref):
    heads = read_ref.shape[0]
    half = max(1, heads // 2)
    return jnp.concatenate([read_ref[spot(i // half, i % half, half)] for i in range(heads)], axis=1)


def project_own_kernel(column_ref, read_ref, weight_ref, sum_ref, *refs):
    rest_refs, (own_ref, sems) = refs[:-2], refs[-2:]
    depth, columns = own_ref.shape
    size = weight_ref.shape[0] // depth
    shares = sems.shape[1]
    length = depth // shares
    copies = []
    for s, target in enumerate((own_ref, *rest_refs)):
        base = lax.rem(column_ref[0] + size - s, size) * depth
        for i in range(shares):
            rows = pl.ds(pl.multiple_of(base + i * length, length), length)
            part = target.at[pl.ds(i * length, length)]
            copies.append(pltpu.make_async_copy(weight_ref.at[rows], part, sems.at[s, i]))
            copies[-1].start()
    flat = flat_heads(read_ref)
    for i in range(shares):
        copies[i].wait()
        rows = slice(i * length, (i + 1) * length)
        value = dot(flat[:, rows], own_ref[rows])
        sum_ref[...] = value if i == 0 else sum_ref[...] + value
    for copy in copies[shares:]:
        copy.wait()


def project_rest_kernel(sum_ref, *refs):
    refs, (out_ref, held_ref, sems) = refs[:-3], refs[-3:]
    reads, weights = refs[: len(refs) // 2], refs[len(refs) // 2 :]
    flats = [flat_heads(read) for read in reads]
    shares = sems.shape[0]
    width = held_ref.shape[1] // shares
    copies = []
    for i in range(shares):
        columns = pl.ds(i * width, width)
        value = sum_ref[:, columns]
        for flat, weight in zip(flats, weights):
            value = value + dot(flat, weight[:, columns])
        held_ref[:, columns] = (value * sigmoid(value)).astype(BF16)
        copies.append(
            pltpu.make_async_copy(held_ref.at[:, columns], out_ref.at[:, columns], sems.at[i])
        )
        copies[-1].start()
    for copy in copies:
        copy.wait()


def call(kernel, out_shape, args, scalars=0, flops=None, limit=12, hbm=(), scratch=()):
    specs = [pl.BlockSpec(memory_space=pltpu.SMEM)] * scalars
    specs += [
        pl.BlockSpec(memory_space=pl.ANY if i in hbm else pltpu.VMEM)
        for i in range(scalars, len(args))
    ]
    cost = None
    if flops is not None:
        cost = pl.CostEstimate(flops=flops, bytes_accessed=2**20, transcendentals=0)
    return pl.pallas_call(
        kernel,
        out_shape=out_shape,
        in_specs=specs,
        out_specs=jax.tree.map(
            lambda _: pl.BlockSpec(memory_space=pl.ANY if -1 in hbm else pltpu.VMEM), out_shape
        ),
        scratch_shapes=list(scratch),
        compiler_params=pltpu.CompilerParams(vmem_limit_bytes=limit * 2**20),
        cost_estimate=cost,
    )(*args)


def on_device(tok_size, head_size, keys, values, queries, fast_weights, step_size, edit_mask, out_proj):
    tokens = keys.shape[0]
    kinds, heads, dh, ff = fast_weights.shape
    column = lax.axis_index("head")
    place = lax.axis_index("tok")
    count = tok_size // heads
    struct = jax.ShapeDtypeStruct
    both = ("tok", "head")

    quarter = tok_size // 4
    mixed = count == 2 and quarter * 4 == tok_size and head_size % 2 == 0
    slot = place % heads
    groups, turn = [], []
    for h in range(head_size):
        if mixed and h % 2 == 1:
            order = [q * quarter + i for q in (0, 2, 1, 3) for i in range(quarter)]
            partners = [t + quarter if t // quarter % 2 == 0 else t - quarter for t in range(tok_size)]
        else:
            order = list(range(tok_size))
            partners = [(t + heads) % tok_size for t in range(tok_size)]
        for g in range(count):
            groups.append([t * head_size + h for t in order[g * heads : (g + 1) * heads]])
        turn += [(t * head_size + h, partners[t] * head_size + h) for t in range(tok_size)]
    if mixed:
        other = place % quarter + quarter * (place // (2 * quarter))
        slot = jnp.where(column % 2 == 1, other, slot)
    turned = heads // 2
    groups = [g[turned:] + g[:turned] for g in groups]
    slot = (slot + heads - turned) % heads

    pairs = call(
        pack_kernel,
        struct((heads, 2, tokens, dh), BF16),
        (edit_mask[None], keys, values),
        hbm=(-1, 0, 1, 2),
        limit=60,
        scratch=[
            pltpu.VMEM((2, tokens, heads * dh), BF16),
            pltpu.VMEM((heads, 2, tokens, dh), BF16),
            pltpu.VMEM((1, *edit_mask.shape), edit_mask.dtype),
            pltpu.SemaphoreType.DMA((2, 2)),
            pltpu.SemaphoreType.DMA((2, 2)),
            pltpu.SemaphoreType.DMA,
        ],
    )
    received = lax.all_to_all(pairs, both, 0, 0, tiled=True, axis_index_groups=groups)
    packed = queries.reshape(tokens, heads, dh).transpose(1, 0, 2)
    half = max(1, heads // 2)
    side = slot // half
    halves_of = [g[i : i + half] for g in groups for i in range(0, heads, half)]
    across = [(g[i], g[(i + half) % heads]) for g in groups for i in range(heads)]
    theirs = lax.dynamic_slice_in_dim(packed, (1 - side) * half, half, 0)
    theirs = lax.ppermute(theirs, both, across)
    mine = lax.dynamic_slice_in_dim(packed, side * half, half, 0)
    asked = call(merge_kernel, struct((half, 2, tokens, dh), BF16), (mine, theirs))
    weights = lax.dynamic_index_in_dim(fast_weights, slot, 1, keepdims=False)
    chunk = max(c for c in (1, 2, 4) if heads % c == 0)
    split = 2 if ff % (2 * LANES) == 0 else 1
    width = ff // split
    low = weights.astype(BF16)
    coded = count == 2
    partials = []
    for start in range(0, ff, width):
        sums = struct((kinds, dh, width), F32)
        rows = kinds * dh * width // LANES + code_rows(kinds * width // LANES)
        partial = call(
            functools.partial(gradient_kernel, max(1, chunk // 2), start),
            struct((rows, LANES), jnp.int16) if coded else sums,
            (received, low),
            flops=2**32,
            limit=16,
            scratch=[pltpu.VMEM(sums.shape, F32)] if coded else [],
        )
        partials.append(partial)

    asked = lax.all_to_all(asked, both, 0, 0, tiled=True, axis_index_groups=halves_of)
    if coded:
        parts = [x for code in partials for x in (code, lax.ppermute(code, both, turn))]
    else:
        same = [[g * heads + i for g in range(count)] for i in range(heads)]
        parts = lax.psum(tuple(partials), "tok", axis_index_groups=same)
    new = call(
        functools.partial(update_kernel, ITERS, coded),
        struct((kinds, dh, ff), BF16),
        (slot.reshape(1), step_size, *parts, weights),
        scalars=2,
        flops=2**33,
    )
    read = call(
        functools.partial(read_kernel, 1),
        struct((heads, tokens, dh), BF16),
        (side.reshape(1), new, asked),
        scalars=1,
        limit=16,
    )

    places = sorted(range(heads), key=lambda i: spot(i // half, i % half, half))
    reads = lax.all_to_all(
        read, both, 0, 0, tiled=True, axis_index_groups=[[g[i] for i in places] for g in groups]
    )
    pieces = [
        lax.ppermute(reads, "head", [(i, (i + s) % head_size) for i in range(head_size)])
        for s in range(1, head_size)
    ]
    columns = out_proj.shape[1]
    depth = heads * dh
    parts_of = max(c for c in (1, 2, 4) if depth % (c * LANES) == 0)
    own, *rest = call(
        project_own_kernel,
        (
            struct((tokens, columns), F32),
            *[struct((depth, columns), BF16) for _ in range(1, head_size)],
        ),
        (column.reshape(1), reads, out_proj),
        scalars=1,
        hbm=(2,),
        limit=49,
        scratch=[pltpu.VMEM((depth, columns), BF16), pltpu.SemaphoreType.DMA((head_size, parts_of))],
    )
    shares = max(c for c in (1, 2, 4) if columns % (c * LANES) == 0)
    return call(
        project_rest_kernel,
        struct((tokens, columns), BF16),
        (own, *pieces, *rest),
        hbm=(-1,),
        scratch=[pltpu.VMEM((tokens, columns), BF16), pltpu.SemaphoreType.DMA((shares,))],
    )


def solution(mesh):
    sizes = dict(mesh.shape)
    in_specs = (
        P("tok", "head"),
        P("tok", "head"),
        P("tok", "head"),
        P(None, "head", None, None),
        P("head"),
        P("tok"),
        P(None, "head"),
    )
    return jax.shard_map(
        functools.partial(on_device, sizes["tok"], sizes["head"]),
        mesh=mesh,
        in_specs=in_specs,
        out_specs=P("tok", "head"),
        check_vma=False,
    )
```
